32 devices in a mesh: dp: 8 (over z, y), tm: 4 (over x, core).
Axes of the slice: x: 2, y: 2, z: 4, core: 2. Of those that a mesh axis runs over, the one named last changes fastest.
Arguments:
- frames: bfloat16 [8, 1024, 1536], P('dp', 'tm'), may hold values from -6 to 6
- lengths: int32 [8], P('dp'), may hold values from 256 to 1024
- ln_gain: float32 [1536], replicated, may hold values from 0.1 to 1.9
- w_query: bfloat16 [1536, 768], P('dp'), may hold values from -0.15625 to 0.15625
- w_key: bfloat16 [1536, 768], P('dp'), may hold values from -0.15625 to 0.15625
- w_value: bfloat16 [1536, 768], P('dp'), may hold values from -0.15625 to 0.15625
- w_output: bfloat16 [768, 1536], P('dp'), may hold values from -0.21875 to 0.21875
- w_position: bfloat16 [1536, 768], P(None, 'tm'), may hold values from -0.15625 to 0.15625
- bias_content: float32 [8, 96], replicated, may hold values from -60 to 60, as said below
- bias_position: float32 [8, 96], replicated, may hold values from -3 to 3
Outputs:
- attended: bfloat16 [8, 1024, 1536], P('dp', 'tm')
The draws below stay inside these ranges and needn't reach their ends.
Inputs may be any that keep to these rules, and one draw needn't show every extreme that they name: `lengths`: number of valid frames of each utterance; later frames are padding. `bias_content`: content biases; in some draws they reach magnitudes near 60.
All inputs are finite; a program needn't handle non-finite values.
Results may differ from the reference program's by a relative error of at most 0.012.
The reference program's roundings to bfloat16 on the way count: a program that leaves them out, or rounds other values in their place, can miss the bound.
Values may be sent and summed in bfloat16 or wider, within the bound.
No kernel may reach another device: no remote copies, remote signals or barrier semaphores. Data moves between devices by JAX's collectives and lax.ppermute only.
A program may use at most 64 MiB of HBM per device.

```python
import math
import jax
import jax.numpy as jnp
from jax import lax

D = 1536
HEADS = 8
HS = 96
UTTS = 8
NT = 1024
HD = 768
N_TM = 4


def draw_bias_content(key, part):
    return jnp.clip(0.5 * jax.random.normal(key, (HEADS, HS), jnp.float32), -3.0, 3.0)


def place_ends(values, stream_key, low, top_value):
    longest = values.shape.index(max(values.shape))
    spots = []
    for shift in (0, 1):
        where = [jax.random.randint(jax.random.fold_in(stream_key, axis), (), 0, length) for axis, length in enumerate(values.shape)]
        where[longest] = (where[longest] + shift) % values.shape[longest]
        spots.append(tuple(where))
    return values.at[spots[0]].set(low).at[spots[1]].set(top_value)


def block_levels(stream_key, dims, shards, least, largest):
    def one(dim, parts):
        draws = jax.random.uniform(jax.random.fold_in(jax.random.fold_in(stream_key, 6), dim), (parts,), jnp.float32, least / len(shards), largest / len(shards))
        return jnp.repeat(jnp.exp(draws), dims[dim] // parts).reshape((-1,) + (1,) * (len(dims) - dim - 1))

    gain = one(*shards[0])
    for cut in shards[1:]:
        gain = gain * one(*cut)
    return gain


def noise(key, extent, deviation, most, shards=(), kind=jnp.bfloat16):
    factor_of = block_levels(key, extent, shards, -0.22, 0.18) if shards else 1.0
    entries = jax.random.normal(key, extent, jnp.float32) * deviation * factor_of
    return jnp.minimum(jnp.maximum(entries, -most), most).astype(kind)


def setup_inputs(seed: int = 0) -> dict:
    seeds = jax.random.split(jax.random.key(seed), 11)
    frames = noise(seeds[0], (UTTS, NT, D), 1.0, 6.0, ((0, 8), (1, 4)))
    lengths = place_ends(jax.random.randint(seeds[1], (UTTS,), NT // 4, NT + 1), jax.random.fold_in(seeds[1], 1), NT // 4, NT).astype(jnp.int32)
    ln_gain = jnp.clip(1.0 + 0.18 * jax.random.normal(seeds[2], (D,), jnp.float32), 0.1, 1.9)
    w_query = noise(seeds[3], (D, HD), D ** -0.5, 0.15625, ((0, 8),))
    w_key = noise(seeds[4], (D, HD), D ** -0.5, 0.15625, ((0, 8),))
    w_value = noise(seeds[5], (D, HD), D ** -0.5, 0.15625, ((0, 8),))
    w_output = noise(seeds[6], (HD, D), HD ** -0.5, 0.21875, ((0, 8),))
    w_position = noise(seeds[7], (D, HD), D ** -0.5, 0.15625, ((1, 4),))
    bias_content = draw_bias_content(jax.random.fold_in(seeds[10], 71), 0)
    bias_position = noise(seeds[9], (HEADS, HS), 0.5, 3.0, (), jnp.float32)
    return {"frames": frames, "lengths": lengths, "ln_gain": ln_gain, "w_query": w_query, "w_key": w_key, "w_value": w_value, "w_output": w_output, "w_position": w_position, "bias_content": bias_content, "bias_position": bias_position}


epsilon = 1e-05
masked_score = -1e+30

def layer_norm(frame_rows, ln_gain):
    widened = frame_rows.astype(jnp.float32)
    row_mean = lax.optimization_barrier(jnp.mean(widened, axis=-1, keepdims=True))
    centered = widened - row_mean
    row_var = lax.optimization_barrier(jnp.mean(centered * centered, axis=-1, keepdims=True))
    return (centered * lax.rsqrt(row_var + epsilon) * ln_gain).astype(jnp.bfloat16)

def sinusoid(row_count, model_width):
    offsets = jnp.arange(row_count, dtype=jnp.float32) - (row_count // 2 - 1)
    half_width = model_width // 2
    frequency = jnp.exp(jnp.arange(half_width, dtype=jnp.float32) * (-2.0 * math.log(10000.0) / model_width))
    angles = offsets[:, None] * frequency[None, :]
    return jnp.concatenate([jnp.sin(angles), jnp.cos(angles)], axis=1).astype(jnp.bfloat16)

def rel_shift(position_full):
    block_len = position_full.shape[0]
    span_len = position_full.shape[1]
    skewed = position_full.reshape(-1)[:block_len * (span_len - 1)].reshape(block_len, span_len - 1)
    return skewed[:, block_len - 1:4 * block_len - 1]

def attend(query_proj, key_rows, value_rows, rel_heads, bias_content, bias_position, valid_len, first_pos):
    block_len = query_proj.shape[0]
    head_count, head_size = bias_content.shape
    query_pos = first_pos + jnp.arange(block_len, dtype=jnp.int32)
    key_pos = first_pos - block_len + jnp.arange(3 * block_len, dtype=jnp.int32)
    key_valid = (key_pos >= 0) & (key_pos < valid_len)
    query_valid = (query_pos < valid_len).astype(jnp.float32)
    split_query = query_proj.reshape(block_len, head_count, head_size).astype(jnp.float32)
    with_content = (split_query + bias_content[None]).astype(jnp.bfloat16).transpose(1, 0, 2)
    with_position = (split_query + bias_position[None]).astype(jnp.bfloat16).transpose(1, 0, 2)
    key_heads = key_rows.reshape(3 * block_len, head_count, head_size).transpose(1, 0, 2)
    value_heads = value_rows.reshape(3 * block_len, head_count, head_size).transpose(1, 0, 2)
    scale = 1.0 / math.sqrt(head_size)

    def one_head(operands):
        content_query, position_query, key_head, value_head, rel_head = operands
        content = jnp.dot(content_query, key_head.T, preferred_element_type=jnp.float32)
        shifted = rel_shift(jnp.dot(position_query, rel_head.T, preferred_element_type=jnp.float32))
        scores = jnp.where(key_valid[None, :], (content + shifted) * scale, masked_score)
        row_max = lax.optimization_barrier(jnp.max(scores, axis=1, keepdims=True))
        raised = jnp.exp(scores - row_max)
        totals = lax.optimization_barrier(jnp.sum(raised, axis=1, keepdims=True))
        weights = (raised / totals).astype(jnp.bfloat16)
        return jnp.dot(weights, value_head, preferred_element_type=jnp.float32)
    context = lax.map(one_head, (with_content, with_position, key_heads, value_heads, rel_heads))
    context = context.transpose(1, 0, 2) * query_valid[:, None, None]
    return context.astype(jnp.bfloat16).reshape(block_len, head_count * head_size)

def reference(frames, lengths, ln_gain, w_query, w_key, w_value, w_output, w_position, bias_content, bias_position):
    total_len = frames.shape[1]
    model_width = frames.shape[2]
    block_len = total_len // N_TM
    head_count, head_size = bias_content.shape
    relative = jnp.dot(sinusoid(4 * block_len, model_width), w_position, preferred_element_type=jnp.float32).astype(jnp.bfloat16)
    rel_heads = relative.reshape(4 * block_len, head_count, head_size).transpose(1, 0, 2)

    def one_utterance(operands):
        frame_rows, valid_len = operands
        normed = layer_norm(frame_rows, ln_gain)
        query_proj = jnp.dot(normed, w_query, preferred_element_type=jnp.float32).astype(jnp.bfloat16)
        key_proj = jnp.dot(normed, w_key, preferred_element_type=jnp.float32).astype(jnp.bfloat16)
        value_proj = jnp.dot(normed, w_value, preferred_element_type=jnp.float32).astype(jnp.bfloat16)
        key_padded = jnp.pad(key_proj, ((block_len, block_len), (0, 0)))
        value_padded = jnp.pad(value_proj, ((block_len, block_len), (0, 0)))

        def one_block(block_idx):
            first_pos = block_idx * block_len
            return attend(lax.dynamic_slice_in_dim(query_proj, first_pos, block_len, 0), lax.dynamic_slice_in_dim(key_padded, first_pos, 3 * block_len, 0), lax.dynamic_slice_in_dim(value_padded, first_pos, 3 * block_len, 0), rel_heads, bias_content, bias_position, valid_len, first_pos)
        context = lax.map(one_block, jnp.arange(N_TM, dtype=jnp.int32)).reshape(total_len, head_count * head_size)
        mixed_out = jnp.dot(context, w_output, preferred_element_type=jnp.float32)
        return (frame_rows.astype(jnp.float32) + mixed_out).astype(jnp.bfloat16)
    return lax.map(one_utterance, (frames, lengths))
```

```python
import functools
import math

import jax
import jax.numpy as jnp
from jax import lax
from jax.experimental import pallas as pl
from jax.experimental.pallas import tpu as pltpu
from jax.sharding import PartitionSpec as P

epsilon = 1e-05
masked_score = -1e30


def padded(block, sides, width):
    for axis, dim in sides:
        count = lax.axis_size(axis)
        forward = [(i, i + 1) for i in range(count - 1)]
        backward = [(target, source) for source, target in forward]
        low = lax.ppermute(
            lax.slice_in_dim(block, block.shape[dim] - width, None, axis=dim), axis, forward
        )
        high = lax.ppermute(lax.slice_in_dim(block, 0, width, axis=dim), axis, backward)
        block = jnp.concatenate([low, block, high], axis=dim)
    return block


def layer_norm(frame_rows, ln_gain):
    widened = frame_rows.astype(jnp.float32)
    row_mean = jnp.mean(widened, axis=-1, keepdims=True)
    centered = widened - row_mean
    row_var = jnp.mean(centered * centered, axis=-1, keepdims=True)
    return (centered * lax.rsqrt(row_var + epsilon) * ln_gain).astype(jnp.bfloat16)


def sinusoid(row_count, model_width):
    offsets = jnp.arange(row_count, dtype=jnp.float32) - (row_count // 2 - 1)
    half_width = model_width // 2
    frequency = jnp.exp(
        jnp.arange(half_width, dtype=jnp.float32) * (-2.0 * math.log(10000.0) / model_width)
    )
    angles = offsets[:, None] * frequency[None, :]
    return jnp.concatenate([jnp.sin(angles), jnp.cos(angles)], axis=1).astype(jnp.bfloat16)


def rel_shift(position_full):
    block_len = position_full.shape[0]
    span_len = position_full.shape[1]
    skewed = position_full.reshape(-1)[: block_len * (span_len - 1)].reshape(
        block_len, span_len - 1
    )
    return skewed[:, block_len - 1 : 4 * block_len - 1]


def attend(
    query_proj, key_rows, value_rows, rel_heads, bias_content, bias_position, valid_len, first_pos
):
    block_len = query_proj.shape[0]
    head_count, head_size = bias_content.shape
    query_pos = first_pos + jnp.arange(block_len, dtype=jnp.int32)
    key_pos = first_pos - block_len + jnp.arange(3 * block_len, dtype=jnp.int32)
    key_valid = (key_pos >= 0) & (key_pos < valid_len)
    query_valid = (query_pos < valid_len).astype(jnp.float32)
    split_query = query_proj.reshape(block_len, head_count, head_size).astype(jnp.float32)
    with_content = (split_query + bias_content[None]).astype(jnp.bfloat16).transpose(1, 0, 2)
    with_position = (split_query + bias_position[None]).astype(jnp.bfloat16).transpose(1, 0, 2)
    key_heads = key_rows.reshape(3 * block_len, head_count, head_size).transpose(1, 0, 2)
    value_heads = value_rows.reshape(3 * block_len, head_count, head_size).transpose(1, 0, 2)
    scale = 1.0 / math.sqrt(head_size)

    def one_head(operands):
        content_query, position_query, key_head, value_head, rel_head = operands
        content = jnp.dot(content_query, key_head.T, preferred_element_type=jnp.float32)
        shifted = rel_shift(jnp.dot(position_query, rel_head.T, preferred_element_type=jnp.float32))
        scores = jnp.where(key_valid[None, :], (content + shifted) * scale, masked_score)
        row_max = jnp.max(scores, axis=1, keepdims=True)
        raised = jnp.exp(scores - row_max)
        totals = jnp.sum(raised, axis=1, keepdims=True)
        weights = (raised / totals).astype(jnp.bfloat16)
        return jnp.dot(weights, value_head, preferred_element_type=jnp.float32)

    context = lax.map(one_head, (with_content, with_position, key_heads, value_heads, rel_heads))
    context = context.transpose(1, 0, 2) * query_valid[:, None, None]
    return context.astype(jnp.bfloat16).reshape(block_len, head_count * head_size)


def column_cut(weight_shard, tm_index, tm_count):
    slice_width = weight_shard.shape[1] // tm_count
    return lax.dynamic_slice_in_dim(weight_shard, tm_index * slice_width, slice_width, 1)


def body_blocks(
    frames,
    lengths,
    ln_gain,
    w_query,
    w_key,
    w_value,
    w_output,
    w_position,
    bias_content,
    bias_position,
):
    frame_rows = frames[0]
    valid_len = lengths[0]
    block_len = frame_rows.shape[0]
    model_width = frame_rows.shape[1]
    head_count, head_size = bias_content.shape
    tm_index = lax.axis_index("tm")
    first_pos = tm_index * block_len
    normed = layer_norm(frame_rows, ln_gain)
    rel_share = jnp.dot(
        sinusoid(4 * block_len, model_width), w_position, preferred_element_type=jnp.float32
    ).astype(jnp.bfloat16)
    relative = lax.all_gather(rel_share, "tm", axis=1, tiled=True)
    rel_heads = relative.reshape(4 * block_len, head_count, head_size).transpose(1, 0, 2)
    tm_count = lax.axis_size("tm")
    slice_query, slice_key, slice_value, slice_output = (
        lax.all_gather(column_cut(w_query, tm_index, tm_count), "dp", axis=0, tiled=True),
        lax.all_gather(column_cut(w_key, tm_index, tm_count), "dp", axis=0, tiled=True),
        lax.all_gather(column_cut(w_value, tm_index, tm_count), "dp", axis=0, tiled=True),
        lax.all_gather(column_cut(w_output, tm_index, tm_count), "dp", axis=0, tiled=True),
    )
    full_query, full_key, full_value, full_output = (
        lax.all_gather(slice_query, "tm", axis=1, tiled=True),
        lax.all_gather(slice_key, "tm", axis=1, tiled=True),
        lax.all_gather(slice_value, "tm", axis=1, tiled=True),
        lax.all_gather(slice_output, "tm", axis=1, tiled=True),
    )
    query_sum = jnp.dot(normed, full_query, preferred_element_type=jnp.float32)
    key_sum = jnp.dot(normed, full_key, preferred_element_type=jnp.float32)
    value_sum = jnp.dot(normed, full_value, preferred_element_type=jnp.float32)
    query_proj = query_sum.astype(jnp.bfloat16)
    key_proj = key_sum.astype(jnp.bfloat16)
    value_proj = value_sum.astype(jnp.bfloat16)
    stacked = jnp.stack((key_proj, value_proj))
    widened = padded(stacked, (("tm", 1),), block_len)
    key_rows = widened[0]
    value_rows = widened[1]
    context = attend(
        query_proj,
        key_rows,
        value_rows,
        rel_heads,
        bias_content,
        bias_position,
        valid_len,
        first_pos,
    )
    mixed_out = jnp.dot(context, full_output, preferred_element_type=jnp.float32)
    attended = (frame_rows.astype(jnp.float32) + mixed_out).astype(jnp.bfloat16)
    return attended[None]


lanes = 128
whole = pl.BlockSpec(memory_space=pltpu.VMEM)
scalars = pl.BlockSpec(memory_space=pltpu.SMEM)


def call(kernel, out_shape, args, scratch=(), flops=0, data=0):
    return pl.pallas_call(
        kernel,
        out_shape=out_shape,
        in_specs=[scalars] + [whole] * (len(args) - 1),
        out_specs=jax.tree.map(lambda _: whole, out_shape),
        scratch_shapes=list(scratch),
        cost_estimate=pl.CostEstimate(flops=flops, bytes_accessed=data, transcendentals=0),
        compiler_params=pltpu.CompilerParams(vmem_limit_bytes=48 * 1024 * 1024),
    )(*args)


def swap(block, axis, distance):
    count = lax.axis_size(axis)
    return lax.ppermute(block, axis, [(i, i ^ distance) for i in range(count)])


def gather_pieces(block, axis):
    count = lax.axis_size(axis)
    pieces = {0: block}
    for far in range(2, count, 2):
        pieces[far] = swap(block, axis, far)
    for far in range(0, count, 2):
        pieces[far ^ 1] = swap(pieces[far], axis, 1)
    return [pieces[k] for k in range(count)]


def cut_kernel(tm_count, info, query_ref, key_ref, value_ref, out_ref, cut_ref, half_ref):
    width = query_ref.shape[1] // tm_count
    half_width = half_ref.shape[1]
    for index in range(tm_count):

        @pl.when(info[0] == index)
        def _():
            for part, ref in enumerate((query_ref, key_ref, value_ref)):
                cut_ref[:, part * width : (part + 1) * width] = ref[
                    :, index * width : (index + 1) * width
                ]
            side = (index % 2) * half_width
            half_ref[...] = out_ref[:, side : side + half_width]


def norm_kernel(info, frame_ref, gain_ref, normed_ref):
    normed_ref[...] = layer_norm(frame_ref[...], gain_ref[...])


def stack_kernel(count, info, *refs):
    out_ref = refs[count]
    rows = refs[0].shape[0]
    for k in range(count):
        start = pl.multiple_of((info[1] ^ k) * rows, 16)
        out_ref[pl.ds(start, rows), :] = refs[k][...]


def heads_kernel(tm_count, dp_count, head_size, info, *refs):
    normed_refs, refs = refs[:tm_count], refs[tm_count:]
    cut_refs, refs = refs[:dp_count], refs[dp_count:]
    rel_ref, content_ref, position_ref = refs[:3]
    context_refs = refs[3 : 3 + tm_count]
    weight, relative, biases, query, key, value = refs[3 + tm_count :]
    block_len = normed_refs[0].shape[0]
    rows, cut_width = cut_refs[0].shape
    width = cut_width // 3
    head_count = width // head_size
    wide = query.shape[1]
    tm_index, dp_index, valid_len = info[0], info[1], info[2]

    weight[...] = jnp.zeros_like(weight)
    relative[...] = jnp.zeros_like(relative)
    biases[...] = jnp.zeros_like(biases)
    for h in range(head_count):
        spot = slice(h * lanes, h * lanes + head_size)
        relative[:, spot] = rel_ref[:, h * head_size : (h + 1) * head_size]
        row = pl.ds(tm_index * head_count + h, 1)
        biases[0:1, spot] = content_ref[row, :]
        biases[1:2, spot] = position_ref[row, :]
    for k in range(dp_count):
        start = pl.multiple_of((dp_index ^ k) * rows, 16)
        for part in range(3):
            for h in range(head_count):
                source = part * width + h * head_size
                target = part * wide + h * lanes
                weight[pl.ds(start, rows), target : target + head_size] = cut_refs[k][
                    :, source : source + head_size
                ]

    for k in range(tm_count):
        start = pl.multiple_of((tm_index ^ k) * block_len, block_len)
        for part, ref in enumerate((query, key, value)):
            ref[pl.ds(start, block_len), :] = jnp.dot(
                normed_refs[k][...],
                weight[:, part * wide : (part + 1) * wide],
                preferred_element_type=jnp.float32,
            ).astype(jnp.bfloat16)

    scale = 1.0 / math.sqrt(head_size)
    across = (((1,), (1,)), ((), ()))
    for block in range(tm_count):
        low, high = max(block - 1, 0), min(block + 1, tm_count - 1)
        span = (high - low + 1) * block_len
        first = (low - block + 1) * block_len
        heads = []
        for h in range(head_count):
            lane = slice(h * lanes, (h + 1) * lanes)
            widened = query[block * block_len : (block + 1) * block_len, lane].astype(jnp.float32)
            with_content = (widened + biases[0:1, lane]).astype(jnp.bfloat16)
            with_position = (widened + biases[1:2, lane]).astype(jnp.bfloat16)
            keys = slice(low * block_len, (high + 1) * block_len)
            content = lax.dot_general(
                with_content, key[keys, lane], across, preferred_element_type=jnp.float32
            )
            position = lax.dot_general(
                with_position,
                relative[first : first + span + block_len, lane],
                across,
                preferred_element_type=jnp.float32,
            )
            shifted = pltpu.roll(position, span + 1, 1, stride=1, stride_axis=0)[:, :span]
            key_pos = low * block_len + lax.broadcasted_iota(jnp.int32, (1, span), 1)
            scores = jnp.where(key_pos < valid_len, (content + shifted) * scale, masked_score)
            raised = jnp.exp(scores - jnp.max(scores, axis=1, keepdims=True))
            totals = jnp.sum(raised, axis=1, keepdims=True)
            weights = (raised * (1.0 / totals)).astype(jnp.bfloat16)
            context = jnp.dot(weights, value[keys, lane], preferred_element_type=jnp.float32)
            query_pos = block * block_len + lax.broadcasted_iota(jnp.int32, (block_len, 1), 0)
            context = jnp.where(query_pos < valid_len, context, 0.0)
            heads.append(context[:, :head_size].astype(jnp.bfloat16))
        for k in range(tm_count):

            @pl.when((tm_index ^ k) == block)
            def _():
                for h in range(head_count):
                    context_refs[k][:, h * head_size : (h + 1) * head_size] = heads[h]


def out_kernel(tm_count, info, *refs):
    context_refs, (own_ref, other_ref, frame_ref, out_ref) = refs[:tm_count], refs[tm_count:]
    width = context_refs[0].shape[1]
    half_width = own_ref.shape[1]
    for side, ref in enumerate((own_ref, other_ref)):
        lane = pl.ds(pl.multiple_of((lax.rem(info[0], 2) ^ side) * half_width, lanes), half_width)
        total = frame_ref[:, lane].astype(jnp.float32)
        mixed = jnp.zeros_like(total)
        for k in range(tm_count):
            start = pl.multiple_of((info[0] ^ k) * width, 16)
            mixed += jnp.dot(
                context_refs[k][...], ref[pl.ds(start, width), :], preferred_element_type=jnp.float32
            )
        out_ref[:, lane] = (total + mixed).astype(jnp.bfloat16)


def body_heads(
    frames,
    lengths,
    ln_gain,
    w_query,
    w_key,
    w_value,
    w_output,
    w_position,
    bias_content,
    bias_position,
):
    half = jnp.bfloat16
    frame_rows = frames[0]
    block_len, model_width = frame_rows.shape
    head_size = bias_content.shape[1]
    inner_width = w_query.shape[1]
    tm_count, dp_count = lax.axis_size("tm"), lax.axis_size("dp")
    tm_index, dp_index = lax.axis_index("tm"), lax.axis_index("dp")
    info = jnp.stack((tm_index, dp_index, lengths[0])).astype(jnp.int32)
    width = inner_width // tm_count
    wide = width // head_size * lanes

    cut, half_output = call(
        functools.partial(cut_kernel, tm_count),
        (
            jax.ShapeDtypeStruct((w_query.shape[0], 3 * width), half),
            jax.ShapeDtypeStruct((w_output.shape[0], model_width // 2), half),
        ),
        (info, w_query, w_key, w_value, w_output),
    )
    normed = call(
        norm_kernel,
        jax.ShapeDtypeStruct((block_len, model_width), half),
        (info, frame_rows, ln_gain[None]),
    )
    cuts = gather_pieces(cut, "dp")
    normed_all = gather_pieces(normed, "tm")
    relative = jnp.dot(
        sinusoid(4 * block_len, model_width), w_position, preferred_element_type=jnp.float32
    ).astype(half)
    output_pieces = gather_pieces(half_output, "dp")
    total_len = tm_count * block_len
    contexts = call(
        functools.partial(heads_kernel, tm_count, dp_count, head_size),
        [jax.ShapeDtypeStruct((block_len, width), half)] * tm_count,
        (info, *normed_all, *cuts, relative, bias_content, bias_position),
        [
            pltpu.VMEM((model_width, 3 * wide), half),
            pltpu.VMEM((4 * block_len, wide), half),
            pltpu.VMEM((8, wide), jnp.float32),
            pltpu.VMEM((total_len, wide), half),
            pltpu.VMEM((total_len, wide), half),
            pltpu.VMEM((total_len, wide), half),
        ],
    )
    own_output = call(
        functools.partial(stack_kernel, dp_count),
        jax.ShapeDtypeStruct((inner_width, model_width // 2), half),
        (info, *output_pieces),
    )
    other_output = swap(own_output, "tm", 1)
    mine = [contexts[0]] + [swap(contexts[k], "tm", k) for k in range(1, tm_count)]
    attended = call(
        functools.partial(out_kernel, tm_count),
        jax.ShapeDtypeStruct((block_len, model_width), half),
        (info, *mine, own_output, other_output, frame_rows),
    )
    return attended[None]


def body(*args):
    tm_count, dp_count = lax.axis_size("tm"), lax.axis_size("dp")
    head_count, head_size = args[-1].shape
    powers = all(n > 1 and n & (n - 1) == 0 for n in (tm_count, dp_count))
    if powers and head_count % tm_count == 0 and head_size <= lanes:
        return body_heads(*args)
    return body_blocks(*args)


def solution(mesh):
    placed = (
        P("dp", "tm", None),
        P("dp"),
        P(),
        P("dp", None),
        P("dp", None),
        P("dp", None),
        P("dp", None),
        P(None, "tm"),
        P(),
        P(),
    )
    return jax.shard_map(
        body, mesh=mesh, in_specs=placed, out_specs=P("dp", "tm", None), check_vma=False
    )
```

```python
import functools
import math

import jax
import jax.numpy as jnp
from jax import lax
from jax.experimental import pallas as pl
from jax.experimental.pallas import tpu as pltpu
from jax.sharding import PartitionSpec as P

epsilon = 1e-05
masked_score = -1e30


def padded(block, sides, width):
    for axis, dim in sides:
        count = lax.axis_size(axis)
        forward = [(i, i + 1) for i in range(count - 1)]
        backward = [(target, source) for source, target in forward]
        low = lax.ppermute(
            lax.slice_in_dim(block, block.shape[dim] - width, None, axis=dim), axis, forward
        )
        high = lax.ppermute(lax.slice_in_dim(block, 0, width, axis=dim), axis, backward)
        block = jnp.concatenate([low, block, high], axis=dim)
    return block


def layer_norm(frame_rows, ln_gain):
    widened = frame_rows.astype(jnp.float32)
    row_mean = jnp.mean(widened, axis=-1, keepdims=True)
    centered = widened - row_mean
    row_var = jnp.mean(centered * centered, axis=-1, keepdims=True)
    return (centered * lax.rsqrt(row_var + epsilon) * ln_gain).astype(jnp.bfloat16)


def sinusoid(row_count, model_width):
    offsets = jnp.arange(row_count, dtype=jnp.float32) - (row_count // 2 - 1)
    half_width = model_width // 2
    frequency = jnp.exp(
        jnp.arange(half_width, dtype=jnp.float32) * (-2.0 * math.log(10000.0) / model_width)
    )
    angles = offsets[:, None] * frequency[None, :]
    return jnp.concatenate([jnp.sin(angles), jnp.cos(angles)], axis=1).astype(jnp.bfloat16)


def rel_shift(position_full):
    block_len = position_full.shape[0]
    span_len = position_full.shape[1]
    skewed = position_full.reshape(-1)[: block_len * (span_len - 1)].reshape(
        block_len, span_len - 1
    )
    return skewed[:, block_len - 1 : 4 * block_len - 1]


def attend(
    query_proj, key_rows, value_rows, rel_heads, bias_content, bias_position, valid_len, first_pos
):
    block_len = query_proj.shape[0]
    head_count, head_size = bias_content.shape
    query_pos = first_pos + jnp.arange(block_len, dtype=jnp.int32)
    key_pos = first_pos - block_len + jnp.arange(3 * block_len, dtype=jnp.int32)
    key_valid = (key_pos >= 0) & (key_pos < valid_len)
    query_valid = (query_pos < valid_len).astype(jnp.float32)
    split_query = query_proj.reshape(block_len, head_count, head_size).astype(jnp.float32)
    with_content = (split_query + bias_content[None]).astype(jnp.bfloat16).transpose(1, 0, 2)
    with_position = (split_query + bias_position[None]).astype(jnp.bfloat16).transpose(1, 0, 2)
    key_heads = key_rows.reshape(3 * block_len, head_count, head_size).transpose(1, 0, 2)
    value_heads = value_rows.reshape(3 * block_len, head_count, head_size).transpose(1, 0, 2)
    scale = 1.0 / math.sqrt(head_size)

    def one_head(operands):
        content_query, position_query, key_head, value_head, rel_head = operands
        content = jnp.dot(content_query, key_head.T, preferred_element_type=jnp.float32)
        shifted = rel_shift(jnp.dot(position_query, rel_head.T, preferred_element_type=jnp.float32))
        scores = jnp.where(key_valid[None, :], (content + shifted) * scale, masked_score)
        row_max = jnp.max(scores, axis=1, keepdims=True)
        raised = jnp.exp(scores - row_max)
        totals = jnp.sum(raised, axis=1, keepdims=True)
        weights = (raised / totals).astype(jnp.bfloat16)
        return jnp.dot(weights, value_head, preferred_element_type=jnp.float32)

    context = lax.map(one_head, (with_content, with_position, key_heads, value_heads, rel_heads))
    context = context.transpose(1, 0, 2) * query_valid[:, None, None]
    return context.astype(jnp.bfloat16).reshape(block_len, head_count * head_size)


def column_cut(weight_shard, tm_index, tm_count):
    slice_width = weight_shard.shape[1] // tm_count
    return lax.dynamic_slice_in_dim(weight_shard, tm_index * slice_width, slice_width, 1)


def body_blocks(
    frames,
    lengths,
    ln_gain,
    w_query,
    w_key,
    w_value,
    w_output,
    w_position,
    bias_content,
    bias_position,
):
    frame_rows = frames[0]
    valid_len = lengths[0]
    block_len = frame_rows.shape[0]
    model_width = frame_rows.shape[1]
    head_count, head_size = bias_content.shape
    tm_index = lax.axis_index("tm")
    first_pos = tm_index * block_len
    normed = layer_norm(frame_rows, ln_gain)
    rel_share = jnp.dot(
        sinusoid(4 * block_len, model_width), w_position, preferred_element_type=jnp.float32
    ).astype(jnp.bfloat16)
    relative = lax.all_gather(rel_share, "tm", axis=1, tiled=True)
    rel_heads = relative.reshape(4 * block_len, head_count, head_size).transpose(1, 0, 2)
    tm_count = lax.axis_size("tm")
    slice_query, slice_key, slice_value, slice_output = (
        lax.all_gather(column_cut(w_query, tm_index, tm_count), "dp", axis=0, tiled=True),
        lax.all_gather(column_cut(w_key, tm_index, tm_count), "dp", axis=0, tiled=True),
        lax.all_gather(column_cut(w_value, tm_index, tm_count), "dp", axis=0, tiled=True),
        lax.all_gather(column_cut(w_output, tm_index, tm_count), "dp", axis=0, tiled=True),
    )
    full_query, full_key, full_value, full_output = (
        lax.all_gather(slice_query, "tm", axis=1, tiled=True),
        lax.all_gather(slice_key, "tm", axis=1, tiled=True),
        lax.all_gather(slice_value, "tm", axis=1, tiled=True),
        lax.all_gather(slice_output, "tm", axis=1, tiled=True),
    )
    query_sum = jnp.dot(normed, full_query, preferred_element_type=jnp.float32)
    key_sum = jnp.dot(normed, full_key, preferred_element_type=jnp.float32)
    value_sum = jnp.dot(normed, full_value, preferred_element_type=jnp.float32)
    query_proj = query_sum.astype(jnp.bfloat16)
    key_proj = key_sum.astype(jnp.bfloat16)
    value_proj = value_sum.astype(jnp.bfloat16)
    stacked = jnp.stack((key_proj, value_proj))
    widened = padded(stacked, (("tm", 1),), block_len)
    key_rows = widened[0]
    value_rows = widened[1]
    context = attend(
        query_proj,
        key_rows,
        value_rows,
        rel_heads,
        bias_content,
        bias_position,
        valid_len,
        first_pos,
    )
    mixed_out = jnp.dot(context, full_output, preferred_element_type=jnp.float32)
    attended = (frame_rows.astype(jnp.float32) + mixed_out).astype(jnp.bfloat16)
    return attended[None]


lanes = 128
half = jnp.bfloat16
across = (((1,), (1,)), ((), ()))
near = pl.BlockSpec(memory_space=pltpu.VMEM)
far = pl.BlockSpec(memory_space=pl.ANY)
scalars = pl.BlockSpec(memory_space=pltpu.SMEM)


def call(kernel, out_shape, operands, scratch=(), micros=1.0, room=24):
    arrays, specs = zip(*operands)
    return pl.pallas_call(
        kernel,
        out_shape=out_shape,
        in_specs=list(specs),
        out_specs=jax.tree.map(lambda _: near, out_shape),
        scratch_shapes=list(scratch),
        cost_estimate=pl.CostEstimate(
            flops=int(micros * 1.1e9), bytes_accessed=4096, transcendentals=0
        ),
        compiler_params=pltpu.CompilerParams(vmem_limit_bytes=room * 1024 * 1024),
    )(*arrays)


def shaped(*shape):
    return jax.ShapeDtypeStruct(shape, half)


def swap(block, axis, distance):
    count = lax.axis_size(axis)
    return lax.ppermute(block, axis, [(i, i ^ distance) for i in range(count)])


def send_far(block, axis):
    return {0: block} | {k: swap(block, axis, k) for k in range(2, lax.axis_size(axis), 2)}


def send_beside(pieces, axis):
    everything = pieces | {k ^ 1: swap(pieces[k], axis, 1) for k in pieces}
    return [everything[k] for k in sorted(everything)]


def later(value, *others):
    return lax.optimization_barrier((value, *others))[0]


def cut_first_kernel(tm_count, info, query_ref, key_ref, cut_ref):
    width = query_ref.shape[1] // tm_count
    for index in range(tm_count):

        @pl.when(info[0] == index)
        def _():
            columns = slice(index * width, (index + 1) * width)
            cut_ref[:, :width] = query_ref[:, columns]
            cut_ref[:, width:] = key_ref[:, columns]


def cut_second_kernel(tm_count, info, *refs):
    value_ref, cut_ref = refs[0], refs[-1]
    rows = value_ref.shape[0]
    width = value_ref.shape[1] // tm_count
    for index in range(tm_count):

        @pl.when(info[0] == index)
        def _():
            columns = slice(index * width, (index + 1) * width)
            cut_ref[:, :width] = value_ref[: rows // 2, columns]
            cut_ref[:, width:] = value_ref[rows // 2 :, columns]


def cut_output_kernel(info, *refs):
    output_ref, half_ref = refs[0], refs[-1]
    width = half_ref.shape[1]
    start = pl.multiple_of(lax.rem(info[0], 2) * width, lanes)
    half_ref[...] = output_ref[:, pl.ds(start, width)]


def norm_kernel(info, frame_ref, gain_ref, normed_ref):
    normed_ref[...] = layer_norm(frame_ref[...], gain_ref[...])


def angle_tables(row_count, model_width, step):
    half_width = model_width // 2
    frequency = jnp.exp(
        jnp.arange(half_width, dtype=jnp.float32) * (-2.0 * math.log(10000.0) / model_width)
    )
    coarse = jnp.arange(row_count // step, dtype=jnp.float32) * step - (row_count // 2 - 1)
    fine = jnp.arange(step, dtype=jnp.float32)
    angles = jnp.concatenate([coarse, fine])[:, None] * frequency[None, :]
    return jnp.sin(angles), jnp.cos(angles)


def relative_kernel(head_size, step, info, sin_ref, cos_ref, position_ref, rel_ref, encoding):
    row_count, model_width = encoding.shape
    half_width = model_width // 2
    coarse_count = row_count // step
    fine_sin, fine_cos = sin_ref[coarse_count:, :], cos_ref[coarse_count:, :]
    for index in range(coarse_count):
        coarse_sin, coarse_cos = sin_ref[index : index + 1, :], cos_ref[index : index + 1, :]
        rows = slice(index * step, (index + 1) * step)
        encoding[rows, :half_width] = (coarse_sin * fine_cos + coarse_cos * fine_sin).astype(half)
        encoding[rows, half_width:] = (coarse_cos * fine_cos - coarse_sin * fine_sin).astype(half)
    projected = lax.dot_general(
        encoding[...], position_ref[...], across, preferred_element_type=jnp.float32
    ).astype(half)
    rel_ref[...] = jnp.zeros_like(rel_ref)
    for h in range(rel_ref.shape[1] // lanes):
        rel_ref[:, h * lanes : h * lanes + head_size] = projected[
            :, h * head_size : (h + 1) * head_size
        ]


def load(sources, targets, sems):
    copies = [
        pltpu.make_async_copy(source, target, sems.at[i])
        for i, (source, target) in enumerate(zip(sources, targets))
    ]
    for copy in copies:
        copy.start()
    return copies


def query_key_kernel(tm_count, dp_count, head_size, info, *refs):
    normed_refs, refs = refs[:tm_count], refs[tm_count:]
    cut_refs, refs = refs[:dp_count], refs[dp_count:]
    query_ref, key_ref, normed, cuts, weight, cut_sems, normed_sems = refs[1:]
    block_len = normed.shape[0] // tm_count
    rows, cut_width = cuts.shape[1:]
    wide = query_ref.shape[1]
    width = cut_width // 2
    spots = [pl.multiple_of((info[0] ^ k) * block_len, block_len) for k in range(tm_count)]
    cut_copies = load(cut_refs, [cuts.at[k] for k in range(dp_count)], cut_sems)
    normed_copies = load(
        normed_refs, [normed.at[pl.ds(spot, block_len), :] for spot in spots], normed_sems
    )
    weight[...] = jnp.zeros_like(weight)
    for k in range(dp_count):
        cut_copies[k].wait()
        start = pl.multiple_of((info[1] ^ k) * rows, 16)
        for part in range(2):
            for h in range(width // head_size):
                source = part * width + h * head_size
                target = part * wide + h * lanes
                weight[pl.ds(start, rows), target : target + head_size] = cuts[
                    k, :, source : source + head_size
                ]
    for copy in normed_copies:
        copy.wait()
    for part, ref in enumerate((query_ref, key_ref)):
        ref[...] = jnp.dot(
            normed[...],
            weight[:, part * wide : (part + 1) * wide],
            preferred_element_type=jnp.float32,
        ).astype(half)


def softmax_kernel(
    tm_count, info, query, key, relative, content_ref, position_ref, weights_ref, biases
):
    head_count, head_size = weights_ref.shape[1], content_ref.shape[1]
    block_len = weights_ref.shape[2]
    tm_index, valid_len = info[0], info[2]
    biases[...] = jnp.zeros_like(biases)
    for h in range(head_count):
        row = pl.ds(tm_index * head_count + h, 1)
        biases[0:1, h * lanes : h * lanes + head_size] = content_ref[row, :]
        biases[1:2, h * lanes : h * lanes + head_size] = position_ref[row, :]
    scale = 1.0 / math.sqrt(head_size)
    for block in range(tm_count):
        low, high = max(block - 1, 0), min(block + 1, tm_count - 1)
        span = (high - low + 1) * block_len
        first = (low - block + 1) * block_len
        keys = slice(low * block_len, (high + 1) * block_len)
        for h in range(head_count):
            lane = slice(h * lanes, (h + 1) * lanes)
            widened = query[block * block_len : (block + 1) * block_len, lane].astype(jnp.float32)
            with_content = (widened + biases[0:1, lane]).astype(half)
            with_position = (widened + biases[1:2, lane]).astype(half)
            content = lax.dot_general(
                with_content, key[keys, lane], across, preferred_element_type=jnp.float32
            )
            position = lax.dot_general(
                with_position,
                relative[first : first + span + block_len, lane],
                across,
                preferred_element_type=jnp.float32,
            )
            shifted = pltpu.roll(position, span + 1, 1, stride=1, stride_axis=0)[:, :span]
            key_pos = low * block_len + lax.broadcasted_iota(jnp.int32, (1, span), 1)
            scores = jnp.where(key_pos < valid_len, (content + shifted) * scale, masked_score)
            raised = jnp.exp(scores - jnp.max(scores, axis=1, keepdims=True))
            totals = jnp.sum(raised, axis=1, keepdims=True)
            if first > 0:
                weights_ref[block, h, :, :first] = jnp.zeros((block_len, first), half)
            weights_ref[block, h, :, first : first + span] = (raised * (1.0 / totals)).astype(half)
            if first + span < 3 * block_len:
                weights_ref[block, h, :, first + span :] = jnp.zeros(
                    (block_len, 3 * block_len - first - span), half
                )


def mix_values(info, distances, weights_ref, value, context_refs, head_size):
    block_len = weights_ref.shape[2]
    for k, context_ref in zip(distances, context_refs):
        block = info[0] ^ k
        query_pos = block * block_len + lax.broadcasted_iota(jnp.int32, (block_len, 1), 0)
        window = pl.ds(pl.multiple_of(block * block_len, block_len), 3 * block_len)
        width = context_ref.shape[1] // 2
        for h in range(weights_ref.shape[1]):
            context = jnp.dot(
                weights_ref[block, h],
                value[window, h * lanes : (h + 1) * lanes],
                preferred_element_type=jnp.float32,
            )
            context = jnp.where(query_pos < info[2], context, 0.0)[:, :head_size].astype(half)
            for part in range(2):
                lane = part * width + h * head_size
                context_ref[:, lane : lane + head_size] = context[
                    part * (block_len // 2) : (part + 1) * (block_len // 2), :
                ]


def value_kernel(tm_count, dp_count, head_size, distances, info, *refs):
    normed, cut_refs, refs = refs[0], refs[1 : 1 + dp_count], refs[1 + dp_count :]
    weights_ref, value, refs = refs[0], refs[1], refs[2:]
    context_refs, (cuts, weight, cut_sems) = refs[: len(distances)], refs[len(distances) :]
    block_len = normed.shape[0] // tm_count
    rows = cuts.shape[1]
    width = cuts.shape[2] // 2
    cut_copies = load(cut_refs, [cuts.at[k] for k in range(dp_count)], cut_sems)
    weight[...] = jnp.zeros_like(weight)
    value[:block_len, :] = jnp.zeros_like(value[:block_len, :])
    value[(tm_count + 1) * block_len :, :] = jnp.zeros_like(value[:block_len, :])
    for k in range(dp_count):
        cut_copies[k].wait()
        start = pl.multiple_of((info[1] ^ k) * rows * 2, 16)
        for part in range(2):
            for h in range(width // head_size):
                source = part * width + h * head_size
                weight[
                    pl.ds(start + part * rows, rows), h * lanes : h * lanes + head_size
                ] = cuts[k, :, source : source + head_size]
    value[block_len : (tm_count + 1) * block_len, :] = jnp.dot(
        normed[...], weight[...], preferred_element_type=jnp.float32
    ).astype(half)
    mix_values(info, distances, weights_ref, value, context_refs, head_size)


def mix_kernel(head_size, distances, info, weights_ref, value, *context_refs):
    mix_values(info, distances, weights_ref, value, context_refs, head_size)


def stack_kernel(count, info, *refs):
    stacked = refs[count]
    sems = refs[count + 1]
    rows = refs[0].shape[0]
    spots = [pl.multiple_of((info[1] ^ k) * rows, 16) for k in range(count)]
    for copy in load(refs[:count], [stacked.at[pl.ds(spot, rows), :] for spot in spots], sems):
        copy.wait()


def out_kernel(tm_count, info, *refs):
    context_refs, (own_ref, other_ref, frame_ref, out_ref) = refs[:tm_count], refs[tm_count:]
    width = context_refs[0].shape[1] // 2
    half_width = own_ref.shape[1]
    contexts = [
        jnp.concatenate([ref[:, :width], ref[:, width:]], axis=0) for ref in context_refs
    ]
    for side, ref in enumerate((own_ref, other_ref)):
        lane = pl.ds(pl.multiple_of((lax.rem(info[0], 2) ^ side) * half_width, lanes), half_width)
        mixed = jnp.zeros((contexts[0].shape[0], half_width), jnp.float32)
        for k in range(tm_count):
            start = pl.multiple_of((info[0] ^ k) * width, 16)
            mixed += jnp.dot(
                contexts[k], ref[pl.ds(start, width), :], preferred_element_type=jnp.float32
            )
        out_ref[:, lane] = (frame_ref[:, lane].astype(jnp.float32) + mixed).astype(half)


def body_heads(
    frames,
    lengths,
    ln_gain,
    w_query,
    w_key,
    w_value,
    w_output,
    w_position,
    bias_content,
    bias_position,
):
    frame_rows = frames[0]
    block_len, model_width = frame_rows.shape
    head_size = bias_content.shape[1]
    in_rows, inner_width = w_query.shape
    out_rows = w_output.shape[0]
    tm_count, dp_count = lax.axis_size("tm"), lax.axis_size("dp")
    info = jnp.stack((lax.axis_index("tm"), lax.axis_index("dp"), lengths[0])).astype(jnp.int32)
    scalar = (info, scalars)
    width = inner_width // tm_count
    heads = width // head_size
    wide = heads * lanes
    total_len = tm_count * block_len
    row_count = 4 * block_len

    cut_first = call(
        functools.partial(cut_first_kernel, tm_count),
        shaped(in_rows, 2 * width),
        (scalar, (w_query, near), (w_key, near)),
    )
    normed_own = call(
        norm_kernel,
        shaped(block_len, model_width),
        (scalar, (frame_rows, near), (ln_gain[None], near)),
    )
    first_far = send_far(cut_first, "dp")
    normed_far = send_far(normed_own, "tm")
    cut_second = call(
        functools.partial(cut_second_kernel, tm_count),
        shaped(in_rows // 2, 2 * width),
        (scalar, (w_value, near)),
    )
    half_output = call(
        cut_output_kernel, shaped(out_rows, model_width // 2), (scalar, (w_output, near))
    )
    arrived = [first_far[k] for k in range(2, dp_count, 2)]
    second_far = send_far(later(cut_second, *arrived), "dp")
    first_pieces = send_beside(first_far, "dp")
    normed_pieces = send_beside({k: later(x, *arrived) for k, x in normed_far.items()}, "tm")
    second_pieces = send_beside(second_far, "dp")
    output_far = send_far(later(half_output, *first_pieces[1:]), "dp")
    step = 32
    sines, cosines = angle_tables(row_count, model_width, step)
    relative = call(
        functools.partial(relative_kernel, head_size, step),
        shaped(row_count, wide),
        (scalar, (sines, near), (cosines, near), (w_position.T, near)),
        [pltpu.VMEM((row_count, model_width), half)],
        micros=3.0,
    )
    query, key, normed = call(
        functools.partial(query_key_kernel, tm_count, dp_count, head_size),
        (shaped(total_len, wide), shaped(total_len, wide), shaped(total_len, model_width)),
        (
            scalar,
            *((x, far) for x in normed_pieces),
            *((x, far) for x in first_pieces),
            (relative, far),
        ),
        [
            pltpu.VMEM((dp_count, in_rows, 2 * width), half),
            pltpu.VMEM((model_width, 2 * wide), half),
            pltpu.SemaphoreType.DMA((dp_count,)),
            pltpu.SemaphoreType.DMA((tm_count,)),
        ],
        micros=3.0,
    )
    weights = call(
        functools.partial(softmax_kernel, tm_count),
        shaped(tm_count, heads, block_len, 3 * block_len),
        (
            scalar,
            (query, near),
            (key, near),
            (relative, near),
            (bias_content, near),
            (bias_position, near),
        ),
        [pltpu.VMEM((8, wide), jnp.float32)],
        micros=6.0,
    )
    away = range(2, tm_count)
    value, *contexts = call(
        functools.partial(value_kernel, tm_count, dp_count, head_size, away),
        [shaped(total_len + 2 * block_len, wide)]
        + [shaped(block_len // 2, 2 * width)] * len(away),
        (scalar, (normed, near), *((x, far) for x in second_pieces), (weights, near)),
        [
            pltpu.VMEM((dp_count, in_rows // 2, 2 * width), half),
            pltpu.VMEM((model_width, wide), half),
            pltpu.SemaphoreType.DMA((dp_count,)),
        ],
        micros=2.5,
    )
    mine = {k: swap(context, "tm", k) for k, context in zip(away, contexts)}
    own, beside = call(
        functools.partial(mix_kernel, head_size, range(2)),
        [shaped(block_len // 2, 2 * width)] * 2,
        (scalar, (weights, near), (value, near)),
    )
    output_pieces = send_beside({k: later(x, value) for k, x in output_far.items()}, "dp")
    mine[0], mine[1] = own, swap(beside, "tm", 1)
    own_output = call(
        functools.partial(stack_kernel, dp_count),
        shaped(inner_width, model_width // 2),
        (scalar, *((x, far) for x in output_pieces)),
        [pltpu.SemaphoreType.DMA((dp_count,))],
    )
    other_output = swap(own_output, "tm", 1)
    attended = call(
        functools.partial(out_kernel, tm_count),
        shaped(block_len, model_width),
        (
            scalar,
            *((mine[k], near) for k in range(tm_count)),
            (own_output, near),
            (other_output, near),
            (frame_rows, near),
        ),
        micros=2.0,
    )
    return attended[None]


def body(*args):
    tm_count, dp_count = lax.axis_size("tm"), lax.axis_size("dp")
    head_count, head_size = args[-1].shape
    powers = all(n > 1 and n & (n - 1) == 0 for n in (tm_count, dp_count))
    fits = head_size <= lanes and args[3].shape[0] % 32 == 0 and args[6].shape[0] % 16 == 0
    if powers and fits and head_count % tm_count == 0:
        return body_heads(*args)
    return body_blocks(*args)


def solution(mesh):
    placed = (
        P("dp", "tm", None),
        P("dp"),
        P(),
        P("dp", None),
        P("dp", None),
        P("dp", None),
        P("dp", None),
        P(None, "tm"),
        P(),
        P(),
    )
    return jax.shard_map(
        body, mesh=mesh, in_specs=placed, out_specs=P("dp", "tm", None), check_vma=False
    )
```

```python
import functools
import math

import jax
import jax.numpy as jnp
from jax import lax
from jax.experimental import pallas as pl
from jax.experimental.pallas import tpu as pltpu
from jax.sharding import PartitionSpec as P

epsilon = 1e-05
masked_score = -1e30


def padded(block, sides, width):
    for axis, dim in sides:
        count = lax.axis_size(axis)
        forward = [(i, i + 1) for i in range(count - 1)]
        backward = [(target, source) for source, target in forward]
        low = lax.ppermute(
            lax.slice_in_dim(block, block.shape[dim] - width, None, axis=dim), axis, forward
        )
        high = lax.ppermute(lax.slice_in_dim(block, 0, width, axis=dim), axis, backward)
        block = jnp.concatenate([low, block, high], axis=dim)
    return block


def layer_norm(frame_rows, ln_gain):
    widened = frame_rows.astype(jnp.float32)
    row_mean = jnp.mean(widened, axis=-1, keepdims=True)
    centered = widened - row_mean
    row_var = jnp.mean(centered * centered, axis=-1, keepdims=True)
    return (centered * lax.rsqrt(row_var + epsilon) * ln_gain).astype(jnp.bfloat16)


def sinusoid(row_count, model_width):
    offsets = jnp.arange(row_count, dtype=jnp.float32) - (row_count // 2 - 1)
    half_width = model_width // 2
    frequency = jnp.exp(
        jnp.arange(half_width, dtype=jnp.float32) * (-2.0 * math.log(10000.0) / model_width)
    )
    angles = offsets[:, None] * frequency[None, :]
    return jnp.concatenate([jnp.sin(angles), jnp.cos(angles)], axis=1).astype(jnp.bfloat16)


def rel_shift(position_full):
    block_len = position_full.shape[0]
    span_len = position_full.shape[1]
    skewed = position_full.reshape(-1)[: block_len * (span_len - 1)].reshape(
        block_len, span_len - 1
    )
    return skewed[:, block_len - 1 : 4 * block_len - 1]


def attend(
    query_proj, key_rows, value_rows, rel_heads, bias_content, bias_position, valid_len, first_pos
):
    block_len = query_proj.shape[0]
    head_count, head_size = bias_content.shape
    query_pos = first_pos + jnp.arange(block_len, dtype=jnp.int32)
    key_pos = first_pos - block_len + jnp.arange(3 * block_len, dtype=jnp.int32)
    key_valid = (key_pos >= 0) & (key_pos < valid_len)
    query_valid = (query_pos < valid_len).astype(jnp.float32)
    split_query = query_proj.reshape(block_len, head_count, head_size).astype(jnp.float32)
    with_content = (split_query + bias_content[None]).astype(jnp.bfloat16).transpose(1, 0, 2)
    with_position = (split_query + bias_position[None]).astype(jnp.bfloat16).transpose(1, 0, 2)
    key_heads = key_rows.reshape(3 * block_len, head_count, head_size).transpose(1, 0, 2)
    value_heads = value_rows.reshape(3 * block_len, head_count, head_size).transpose(1, 0, 2)
    scale = 1.0 / math.sqrt(head_size)

    def one_head(operands):
        content_query, position_query, key_head, value_head, rel_head = operands
        content = jnp.dot(content_query, key_head.T, preferred_element_type=jnp.float32)
        shifted = rel_shift(jnp.dot(position_query, rel_head.T, preferred_element_type=jnp.float32))
        scores = jnp.where(key_valid[None, :], (content + shifted) * scale, masked_score)
        row_max = jnp.max(scores, axis=1, keepdims=True)
        raised = jnp.exp(scores - row_max)
        totals = jnp.sum(raised, axis=1, keepdims=True)
        weights = (raised / totals).astype(jnp.bfloat16)
        return jnp.dot(weights, value_head, preferred_element_type=jnp.float32)

    context = lax.map(one_head, (with_content, with_position, key_heads, value_heads, rel_heads))
    context = context.transpose(1, 0, 2) * query_valid[:, None, None]
    return context.astype(jnp.bfloat16).reshape(block_len, head_count * head_size)


def column_cut(weight_shard, tm_index, tm_count):
    slice_width = weight_shard.shape[1] // tm_count
    return lax.dynamic_slice_in_dim(weight_shard, tm_index * slice_width, slice_width, 1)


def body_blocks(
    frames,
    lengths,
    ln_gain,
    w_query,
    w_key,
    w_value,
    w_output,
    w_position,
    bias_content,
    bias_position,
):
    frame_rows = frames[0]
    valid_len = lengths[0]
    block_len = frame_rows.shape[0]
    model_width = frame_rows.shape[1]
    head_count, head_size = bias_content.shape
    tm_index = lax.axis_index("tm")
    first_pos = tm_index * block_len
    normed = layer_norm(frame_rows, ln_gain)
    rel_share = jnp.dot(
        sinusoid(4 * block_len, model_width), w_position, preferred_element_type=jnp.float32
    ).astype(jnp.bfloat16)
    relative = lax.all_gather(rel_share, "tm", axis=1, tiled=True)
    rel_heads = relative.reshape(4 * block_len, head_count, head_size).transpose(1, 0, 2)
    tm_count = lax.axis_size("tm")
    slice_query, slice_key, slice_value, slice_output = (
        lax.all_gather(column_cut(w_query, tm_index, tm_count), "dp", axis=0, tiled=True),
        lax.all_gather(column_cut(w_key, tm_index, tm_count), "dp", axis=0, tiled=True),
        lax.all_gather(column_cut(w_value, tm_index, tm_count), "dp", axis=0, tiled=True),
        lax.all_gather(column_cut(w_output, tm_index, tm_count), "dp", axis=0, tiled=True),
    )
    full_query, full_key, full_value, full_output = (
        lax.all_gather(slice_query, "tm", axis=1, tiled=True),
        lax.all_gather(slice_key, "tm", axis=1, tiled=True),
        lax.all_gather(slice_value, "tm", axis=1, tiled=True),
        lax.all_gather(slice_output, "tm", axis=1, tiled=True),
    )
    query_sum = jnp.dot(normed, full_query, preferred_element_type=jnp.float32)
    key_sum = jnp.dot(normed, full_key, preferred_element_type=jnp.float32)
    value_sum = jnp.dot(normed, full_value, preferred_element_type=jnp.float32)
    query_proj = query_sum.astype(jnp.bfloat16)
    key_proj = key_sum.astype(jnp.bfloat16)
    value_proj = value_sum.astype(jnp.bfloat16)
    stacked = jnp.stack((key_proj, value_proj))
    widened = padded(stacked, (("tm", 1),), block_len)
    key_rows = widened[0]
    value_rows = widened[1]
    context = attend(
        query_proj,
        key_rows,
        value_rows,
        rel_heads,
        bias_content,
        bias_position,
        valid_len,
        first_pos,
    )
    mixed_out = jnp.dot(context, full_output, preferred_element_type=jnp.float32)
    attended = (frame_rows.astype(jnp.float32) + mixed_out).astype(jnp.bfloat16)
    return attended[None]


lanes = 128
half = jnp.bfloat16
across = (((1,), (1,)), ((), ()))
near = pl.BlockSpec(memory_space=pltpu.VMEM)
far = pl.BlockSpec(memory_space=pltpu.HBM)
scalars = pl.BlockSpec(memory_space=pltpu.SMEM)


def call(kernel, out_shape, operands, scratch=(), micros=1.0, room=24):
    arrays, specs = zip(*operands)
    return pl.pallas_call(
        kernel,
        out_shape=out_shape,
        in_specs=list(specs),
        out_specs=jax.tree.map(lambda _: near, out_shape),
        scratch_shapes=list(scratch),
        cost_estimate=pl.CostEstimate(
            flops=int(micros * 1.1e9), bytes_accessed=4096, transcendentals=0
        ),
        compiler_params=pltpu.CompilerParams(vmem_limit_bytes=room * 1024 * 1024),
    )(*arrays)


def shaped(*shape):
    return jax.ShapeDtypeStruct(shape, half)


def swap(block, axis, distance):
    count = lax.axis_size(axis)
    return lax.ppermute(block, axis, [(i, i ^ distance) for i in range(count)])


def send_far(block, axis):
    return {0: block} | {k: swap(block, axis, k) for k in range(2, lax.axis_size(axis), 2)}


def send_beside(pieces, axis):
    everything = dict(pieces)
    for k, piece in pieces.items():
        everything[k ^ 1] = swap(piece, axis, 1)
    return [everything[k] for k in sorted(everything)]


def later(value, *others):
    return lax.optimization_barrier((value, *others))[0]


def prepare_kernel(tm_count, info, *refs):
    gain_ref, cut_ref, half_ref, normed_ref, stage, frame, sems = refs[5:]
    rows, width = stage.shape[1], stage.shape[2] // tm_count
    query_ref, key_ref, value_ref = (stage.at[i] for i in range(3))
    half_width = half_ref.shape[1]
    side = pl.ds(pl.multiple_of(lax.rem(info[0], 2) * half_width, lanes), half_width)
    sources = (refs[4], *refs[:3], refs[3].at[:, side])
    copies = load(sources, (frame, query_ref, key_ref, value_ref, half_ref), sems)
    copies[0].wait()
    normed_ref[...] = layer_norm(frame[...], gain_ref[...])
    for copy in copies[1:]:
        copy.wait()
    for index in range(tm_count):

        @pl.when(info[0] == index)
        def _():
            columns = slice(index * width, (index + 1) * width)
            cut_ref[:rows, :width] = query_ref[:, columns]
            cut_ref[:rows, width:] = key_ref[:, columns]
            cut_ref[rows:, :width] = value_ref[: rows // 2, columns]
            cut_ref[rows:, width:] = value_ref[rows // 2 :, columns]


def angle_tables(row_count, model_width, step):
    half_width = model_width // 2
    frequency = jnp.exp(
        jnp.arange(half_width, dtype=jnp.float32) * (-2.0 * math.log(10000.0) / model_width)
    )
    coarse = jnp.arange(row_count // step, dtype=jnp.float32) * step - (row_count // 2 - 1)
    fine = jnp.arange(step, dtype=jnp.float32)
    angles = jnp.concatenate([coarse, fine])[:, None] * frequency[None, :]
    return jnp.sin(angles), jnp.cos(angles)


def relative_kernel(head_size, step, info, sin_ref, cos_ref, position_ref, rel_ref, encoding):
    row_count, model_width = encoding.shape
    half_width = model_width // 2
    coarse_count = row_count // step
    fine_sin, fine_cos = sin_ref[coarse_count:, :], cos_ref[coarse_count:, :]
    for index in range(coarse_count):
        coarse_sin, coarse_cos = sin_ref[index : index + 1, :], cos_ref[index : index + 1, :]
        rows = slice(index * step, (index + 1) * step)
        encoding[rows, :half_width] = (coarse_sin * fine_cos + coarse_cos * fine_sin).astype(half)
        encoding[rows, half_width:] = (coarse_cos * fine_cos - coarse_sin * fine_sin).astype(half)
    projected = lax.dot_general(
        encoding[...], position_ref[...], across, preferred_element_type=jnp.float32
    ).astype(half)
    rel_ref[...] = jnp.zeros_like(rel_ref)
    for h in range(rel_ref.shape[1] // lanes):
        rel_ref[:, h * lanes : h * lanes + head_size] = projected[
            :, h * head_size : (h + 1) * head_size
        ]


def load(sources, targets, sems):
    copies = [
        pltpu.make_async_copy(source, target, sems.at[i])
        for i, (source, target) in enumerate(zip(sources, targets))
    ]
    for copy in copies:
        copy.start()
    return copies


def project_kernel(tm_count, dp_count, head_size, info, *refs):
    normed_refs, refs = refs[:tm_count], refs[tm_count:]
    cut_refs, refs = refs[:dp_count], refs[dp_count:]
    query_ref, key_ref, value_ref, normed, cuts, weight, cut_sems, normed_sems = refs
    block_len = normed.shape[0] // tm_count
    rows, width = cuts.shape[1] * 2 // 3, cuts.shape[2] // 2
    wide = query_ref.shape[1]
    spots = [pl.multiple_of((info[0] ^ k) * block_len, block_len) for k in range(tm_count)]
    cut_copies = load(cut_refs, [cuts.at[k] for k in range(dp_count)], cut_sems)
    normed_copies = load(
        normed_refs, [normed.at[pl.ds(spot, block_len), :] for spot in spots], normed_sems
    )
    weight[...] = jnp.zeros_like(weight)
    value_ref[:block_len, :] = jnp.zeros_like(value_ref[:block_len, :])
    value_ref[(tm_count + 1) * block_len :, :] = jnp.zeros_like(value_ref[:block_len, :])
    for k in range(dp_count):
        cut_copies[k].wait()
        start = pl.multiple_of((info[1] ^ k) * rows, 16)
        for h in range(width // head_size):
            for part in range(2):
                source = part * width + h * head_size
                target = part * wide + h * lanes
                weight[pl.ds(start, rows), target : target + head_size] = cuts[
                    k, :rows, source : source + head_size
                ]
                target = 2 * wide + h * lanes
                weight[
                    pl.ds(start + part * (rows // 2), rows // 2), target : target + head_size
                ] = cuts[k, rows:, source : source + head_size]
    for copy in normed_copies:
        copy.wait()
    shift = slice(block_len, (tm_count + 1) * block_len)
    for part, ref in enumerate((query_ref, key_ref, value_ref.at[shift, :])):
        ref[...] = jnp.dot(
            normed[...],
            weight[:, part * wide : (part + 1) * wide],
            preferred_element_type=jnp.float32,
        ).astype(half)


def softmax_kernel(
    tm_count, info, query, key, relative, content_ref, position_ref, weights_ref, biases
):
    head_count, head_size = weights_ref.shape[1], content_ref.shape[1]
    block_len = weights_ref.shape[2]
    tm_index, valid_len = info[0], info[2]
    biases[...] = jnp.zeros_like(biases)
    for h in range(head_count):
        row = pl.ds(tm_index * head_count + h, 1)
        biases[0:1, h * lanes : h * lanes + head_size] = content_ref[row, :]
        biases[1:2, h * lanes : h * lanes + head_size] = position_ref[row, :]
    scale = 1.0 / math.sqrt(head_size)
    for block in range(tm_count):
        low, high = max(block - 1, 0), min(block + 1, tm_count - 1)
        span = (high - low + 1) * block_len
        first = (low - block + 1) * block_len
        keys = slice(low * block_len, (high + 1) * block_len)
        for h in range(head_count):
            lane = slice(h * lanes, (h + 1) * lanes)
            widened = query[block * block_len : (block + 1) * block_len, lane].astype(jnp.float32)
            with_content = (widened + biases[0:1, lane]).astype(half)
            with_position = (widened + biases[1:2, lane]).astype(half)
            content = lax.dot_general(
                with_content, key[keys, lane], across, preferred_element_type=jnp.float32
            )
            position = lax.dot_general(
                with_position,
                relative[first : first + span + block_len, lane],
                across,
                preferred_element_type=jnp.float32,
            )
            shifted = pltpu.roll(position, span + 1, 1, stride=1, stride_axis=0)[:, :span]
            key_pos = low * block_len + lax.broadcasted_iota(jnp.int32, (1, span), 1)
            scores = jnp.where(key_pos < valid_len, (content + shifted) * scale, masked_score)
            raised = jnp.exp(scores - jnp.max(scores, axis=1, keepdims=True))
            totals = jnp.sum(raised, axis=1, keepdims=True)
            if first > 0:
                weights_ref[block, h, :, :first] = jnp.zeros((block_len, first), half)
            weights_ref[block, h, :, first : first + span] = (raised * (1.0 / totals)).astype(half)
            if first + span < 3 * block_len:
                weights_ref[block, h, :, first + span :] = jnp.zeros(
                    (block_len, 3 * block_len - first - span), half
                )


def mix_values(info, distances, weights_ref, value, context_refs, head_size):
    block_len = weights_ref.shape[2]
    for k, context_ref in zip(distances, context_refs):
        block = info[0] ^ k
        query_pos = block * block_len + lax.broadcasted_iota(jnp.int32, (block_len, 1), 0)
        window = pl.ds(pl.multiple_of(block * block_len, block_len), 3 * block_len)
        width = context_ref.shape[1] // 2
        for h in range(weights_ref.shape[1]):
            context = jnp.dot(
                weights_ref[block, h],
                value[window, h * lanes : (h + 1) * lanes],
                preferred_element_type=jnp.float32,
            )
            context = jnp.where(query_pos < info[2], context, 0.0)[:, :head_size].astype(half)
            for part in range(2):
                lane = part * width + h * head_size
                context_ref[:, lane : lane + head_size] = context[
                    part * (block_len // 2) : (part + 1) * (block_len // 2), :
                ]


def mix_kernel(head_size, distances, info, weights_ref, value, *context_refs):
    rows = weights_ref.shape[2] // 2
    if len(context_refs) == len(distances):
        places = context_refs
    else:
        places = [
            context_refs[i // 2].at[i % 2 * rows : (i % 2 + 1) * rows, :]
            for i in range(len(distances))
        ]
    mix_values(info, distances, weights_ref, value, places, head_size)


def pair_kernel(info, own_ref, beside_ref, pair_ref):
    rows = own_ref.shape[0]
    own = lax.rem(info[1], 2)
    pair_ref[pl.ds(pl.multiple_of(own * rows, 16), rows), :] = own_ref[...]
    pair_ref[pl.ds(pl.multiple_of((1 - own) * rows, 16), rows), :] = beside_ref[...]


def out_kernel(tm_count, pair_count, info, *refs):
    context_refs, refs = refs[:tm_count], refs[tm_count:]
    pair_refs, refs = refs[: 2 * pair_count], refs[2 * pair_count :]
    frame_ref, out_ref, weight, context, sems = refs
    width = context_refs[0].shape[1] // 2
    rows = pair_refs[0].shape[0]
    half_width = weight.shape[2]
    spots = []
    for k in range(pair_count):
        first = ((info[1] // 2) ^ k) * rows
        source = first // width
        spots.append(pl.multiple_of((source ^ info[0]) * width + first - source * width, 16))
    copies = load(
        pair_refs,
        [weight.at[i // pair_count, pl.ds(spot, rows), :] for i, spot in enumerate(spots * 2)],
        sems,
    )
    for k, ref in enumerate(context_refs):
        for part in range(2):
            context[
                part * (context.shape[0] // 2) : (part + 1) * (context.shape[0] // 2),
                k * width : (k + 1) * width,
            ] = ref[:, part * width : (part + 1) * width]
    for side in range(2):
        for copy in copies[side * pair_count : (side + 1) * pair_count]:
            copy.wait()
        lane = pl.ds(pl.multiple_of((lax.rem(info[0], 2) ^ side) * half_width, lanes), half_width)
        mixed = jnp.dot(context[...], weight[side], preferred_element_type=jnp.float32)
        out_ref[:, lane] = (frame_ref[:, lane].astype(jnp.float32) + mixed).astype(half)


def body_heads(
    frames,
    lengths,
    ln_gain,
    w_query,
    w_key,
    w_value,
    w_output,
    w_position,
    bias_content,
    bias_position,
):
    frame_rows = frames[0]
    block_len, model_width = frame_rows.shape
    head_size = bias_content.shape[1]
    in_rows, inner_width = w_query.shape
    out_rows = w_output.shape[0]
    tm_count, dp_count = lax.axis_size("tm"), lax.axis_size("dp")
    info = jnp.stack((lax.axis_index("tm"), lax.axis_index("dp"), lengths[0])).astype(jnp.int32)
    scalar = (info, scalars)
    width = inner_width // tm_count
    heads = width // head_size
    wide = heads * lanes
    total_len = tm_count * block_len
    row_count = 4 * block_len

    cut, half_output, normed_own = call(
        functools.partial(prepare_kernel, tm_count),
        (
            shaped(in_rows // 2 * 3, 2 * width),
            shaped(out_rows, model_width // 2),
            shaped(block_len, model_width),
        ),
        (
            scalar,
            *((x, far) for x in (w_query, w_key, w_value, w_output, frame_rows)),
            (ln_gain, near),
        ),
        [
            pltpu.VMEM((3, in_rows, inner_width), half),
            pltpu.VMEM((block_len, model_width), half),
            pltpu.SemaphoreType.DMA((5,)),
        ],
        room=56,
    )
    cut_far = send_far(cut, "dp")
    pair = call(
        pair_kernel,
        shaped(2 * out_rows, model_width // 2),
        (scalar, (half_output, near), (swap(half_output, "dp", 1), near)),
        micros=0.5,
    )
    cut_pieces = send_beside(cut_far, "dp")
    step = 32
    sines, cosines = angle_tables(row_count, model_width, step)
    relative = call(
        functools.partial(relative_kernel, head_size, step),
        shaped(row_count, wide),
        (scalar, (sines, near), (cosines, near), (w_position.T, near)),
        [pltpu.VMEM((row_count, model_width), half)],
        micros=2.0,
    )
    normed_pieces = send_beside(send_far(normed_own, "tm"), "tm")
    pairs = send_far(later(pair, *[cut_far[k] for k in range(2, dp_count, 2)]), "dp")
    query, key, value = call(
        functools.partial(project_kernel, tm_count, dp_count, head_size),
        (
            shaped(total_len, wide),
            shaped(total_len, wide),
            shaped(total_len + 2 * block_len, wide),
        ),
        (scalar, *((x, far) for x in normed_pieces), *((x, far) for x in cut_pieces)),
        [
            pltpu.VMEM((total_len, model_width), half),
            pltpu.VMEM((dp_count, in_rows // 2 * 3, 2 * width), half),
            pltpu.VMEM((model_width, 3 * wide), half),
            pltpu.SemaphoreType.DMA((dp_count,)),
            pltpu.SemaphoreType.DMA((tm_count,)),
        ],
        micros=6.0,
    )
    weights = call(
        functools.partial(softmax_kernel, tm_count),
        shaped(tm_count, heads, block_len, 3 * block_len),
        (
            scalar,
            (query, near),
            (key, near),
            (relative, near),
            (bias_content, near),
            (bias_position, near),
        ),
        [pltpu.VMEM((8, wide), jnp.float32)],
        micros=5.0,
    )
    away = range(2, tm_count)
    doubles = call(
        functools.partial(mix_kernel, head_size, away),
        [shaped(block_len, 2 * width)] * (len(away) // 2),
        (scalar, (weights, near), (value, near)),
    )
    received = {k: swap(double, "tm", k) for k, double in zip(away[::2], doubles)}
    own, beside = call(
        functools.partial(mix_kernel, head_size, range(2)),
        [shaped(block_len // 2, 2 * width)] * 2,
        (scalar, (weights, near), (value, near)),
    )
    mine = {0: own, 1: swap(beside, "tm", 1)}
    for k, double in received.items():
        mine[k] = double[: block_len // 2]
        mine[k + 1] = swap(double[block_len // 2 :], "tm", 1)
    own_pairs = [pairs[k] for k in sorted(pairs)]
    other_pairs = [swap(later(x, beside), "tm", 1) for x in own_pairs]
    attended = call(
        functools.partial(out_kernel, tm_count, len(own_pairs)),
        shaped(block_len, model_width),
        (
            scalar,
            *((mine[k], near) for k in range(tm_count)),
            *((x, far) for x in own_pairs + other_pairs),
            (frame_rows, near),
        ),
        [
            pltpu.VMEM((2, inner_width, model_width // 2), half),
            pltpu.VMEM((block_len, inner_width), half),
            pltpu.SemaphoreType.DMA((2 * len(own_pairs),)),
        ],
        micros=2.5,
    )
    return attended[None]


def body(*args):
    tm_count, dp_count = lax.axis_size("tm"), lax.axis_size("dp")
    head_count, head_size = args[-1].shape
    powers = all(n > 1 and n & (n - 1) == 0 for n in (tm_count, dp_count))
    fits = head_size <= lanes and args[3].shape[0] % 32 == 0 and args[6].shape[0] % 16 == 0
    aligned = args[3].shape[1] // tm_count % (2 * args[6].shape[0]) == 0
    if powers and fits and aligned and head_count % tm_count == 0:
        return body_heads(*args)
    return body_blocks(*args)


def solution(mesh):
    placed = (
        P("dp", "tm", None),
        P("dp"),
        P(),
        P("dp", None),
        P("dp", None),
        P("dp", None),
        P("dp", None),
        P(None, "tm"),
        P(),
        P(),
    )
    return jax.shard_map(
        body, mesh=mesh, in_specs=placed, out_specs=P("dp", "tm", None), check_vma=False
    )
```

```python
import functools
import math

import jax
import jax.numpy as jnp
from jax import lax
from jax.experimental import pallas as pl
from jax.experimental.pallas import tpu as pltpu
from jax.sharding import PartitionSpec as P

epsilon = 1e-05
masked_score = -1e30


def padded(block, sides, width):
    for axis, dim in sides:
        count = lax.axis_size(axis)
        forward = [(i, i + 1) for i in range(count - 1)]
        backward = [(target, source) for source, target in forward]
        low = lax.ppermute(
            lax.slice_in_dim(block, block.shape[dim] - width, None, axis=dim), axis, forward
        )
        high = lax.ppermute(lax.slice_in_dim(block, 0, width, axis=dim), axis, backward)
        block = jnp.concatenate([low, block, high], axis=dim)
    return block


def layer_norm(frame_rows, ln_gain):
    widened = frame_rows.astype(jnp.float32)
    row_mean = jnp.mean(widened, axis=-1, keepdims=True)
    centered = widened - row_mean
    row_var = jnp.mean(centered * centered, axis=-1, keepdims=True)
    return (centered * lax.rsqrt(row_var + epsilon) * ln_gain).astype(jnp.bfloat16)


def sinusoid(row_count, model_width):
    offsets = jnp.arange(row_count, dtype=jnp.float32) - (row_count // 2 - 1)
    half_width = model_width // 2
    frequency = jnp.exp(
        jnp.arange(half_width, dtype=jnp.float32) * (-2.0 * math.log(10000.0) / model_width)
    )
    angles = offsets[:, None] * frequency[None, :]
    return jnp.concatenate([jnp.sin(angles), jnp.cos(angles)], axis=1).astype(jnp.bfloat16)


def rel_shift(position_full):
    block_len = position_full.shape[0]
    span_len = position_full.shape[1]
    skewed = position_full.reshape(-1)[: block_len * (span_len - 1)].reshape(
        block_len, span_len - 1
    )
    return skewed[:, block_len - 1 : 4 * block_len - 1]


def attend(
    query_proj, key_rows, value_rows, rel_heads, bias_content, bias_position, valid_len, first_pos
):
    block_len = query_proj.shape[0]
    head_count, head_size = bias_content.shape
    query_pos = first_pos + jnp.arange(block_len, dtype=jnp.int32)
    key_pos = first_pos - block_len + jnp.arange(3 * block_len, dtype=jnp.int32)
    key_valid = (key_pos >= 0) & (key_pos < valid_len)
    query_valid = (query_pos < valid_len).astype(jnp.float32)
    split_query = query_proj.reshape(block_len, head_count, head_size).astype(jnp.float32)
    with_content = (split_query + bias_content[None]).astype(jnp.bfloat16).transpose(1, 0, 2)
    with_position = (split_query + bias_position[None]).astype(jnp.bfloat16).transpose(1, 0, 2)
    key_heads = key_rows.reshape(3 * block_len, head_count, head_size).transpose(1, 0, 2)
    value_heads = value_rows.reshape(3 * block_len, head_count, head_size).transpose(1, 0, 2)
    scale = 1.0 / math.sqrt(head_size)

    def one_head(operands):
        content_query, position_query, key_head, value_head, rel_head = operands
        content = jnp.dot(content_query, key_head.T, preferred_element_type=jnp.float32)
        shifted = rel_shift(jnp.dot(position_query, rel_head.T, preferred_element_type=jnp.float32))
        scores = jnp.where(key_valid[None, :], (content + shifted) * scale, masked_score)
        row_max = jnp.max(scores, axis=1, keepdims=True)
        raised = jnp.exp(scores - row_max)
        totals = jnp.sum(raised, axis=1, keepdims=True)
        weights = (raised / totals).astype(jnp.bfloat16)
        return jnp.dot(weights, value_head, preferred_element_type=jnp.float32)

    context = lax.map(one_head, (with_content, with_position, key_heads, value_heads, rel_heads))
    context = context.transpose(1, 0, 2) * query_valid[:, None, None]
    return context.astype(jnp.bfloat16).reshape(block_len, head_count * head_size)


def column_cut(weight_shard, tm_index, tm_count):
    slice_width = weight_shard.shape[1] // tm_count
    return lax.dynamic_slice_in_dim(weight_shard, tm_index * slice_width, slice_width, 1)


def body_blocks(
    frames,
    lengths,
    ln_gain,
    w_query,
    w_key,
    w_value,
    w_output,
    w_position,
    bias_content,
    bias_position,
):
    frame_rows = frames[0]
    valid_len = lengths[0]
    block_len = frame_rows.shape[0]
    model_width = frame_rows.shape[1]
    head_count, head_size = bias_content.shape
    tm_index = lax.axis_index("tm")
    first_pos = tm_index * block_len
    normed = layer_norm(frame_rows, ln_gain)
    rel_share = jnp.dot(
        sinusoid(4 * block_len, model_width), w_position, preferred_element_type=jnp.float32
    ).astype(jnp.bfloat16)
    relative = lax.all_gather(rel_share, "tm", axis=1, tiled=True)
    rel_heads = relative.reshape(4 * block_len, head_count, head_size).transpose(1, 0, 2)
    tm_count = lax.axis_size("tm")
    slice_query, slice_key, slice_value, slice_output = (
        lax.all_gather(column_cut(w_query, tm_index, tm_count), "dp", axis=0, tiled=True),
        lax.all_gather(column_cut(w_key, tm_index, tm_count), "dp", axis=0, tiled=True),
        lax.all_gather(column_cut(w_value, tm_index, tm_count), "dp", axis=0, tiled=True),
        lax.all_gather(column_cut(w_output, tm_index, tm_count), "dp", axis=0, tiled=True),
    )
    full_query, full_key, full_value, full_output = (
        lax.all_gather(slice_query, "tm", axis=1, tiled=True),
        lax.all_gather(slice_key, "tm", axis=1, tiled=True),
        lax.all_gather(slice_value, "tm", axis=1, tiled=True),
        lax.all_gather(slice_output, "tm", axis=1, tiled=True),
    )
    query_sum = jnp.dot(normed, full_query, preferred_element_type=jnp.float32)
    key_sum = jnp.dot(normed, full_key, preferred_element_type=jnp.float32)
    value_sum = jnp.dot(normed, full_value, preferred_element_type=jnp.float32)
    query_proj = query_sum.astype(jnp.bfloat16)
    key_proj = key_sum.astype(jnp.bfloat16)
    value_proj = value_sum.astype(jnp.bfloat16)
    stacked = jnp.stack((key_proj, value_proj))
    widened = padded(stacked, (("tm", 1),), block_len)
    key_rows = widened[0]
    value_rows = widened[1]
    context = attend(
        query_proj,
        key_rows,
        value_rows,
        rel_heads,
        bias_content,
        bias_position,
        valid_len,
        first_pos,
    )
    mixed_out = jnp.dot(context, full_output, preferred_element_type=jnp.float32)
    attended = (frame_rows.astype(jnp.float32) + mixed_out).astype(jnp.bfloat16)
    return attended[None]


lanes = 128
half = jnp.bfloat16
across = (((1,), (1,)), ((), ()))
near = pl.BlockSpec(memory_space=pltpu.VMEM)
far = pl.BlockSpec(memory_space=pltpu.HBM)
scalars = pl.BlockSpec(memory_space=pltpu.SMEM)


def call(kernel, out_shape, operands, scratch=(), micros=1.0, room=24):
    arrays, specs = zip(*operands)
    return pl.pallas_call(
        kernel,
        out_shape=out_shape,
        in_specs=list(specs),
        out_specs=jax.tree.map(lambda _: near, out_shape),
        scratch_shapes=list(scratch),
        cost_estimate=pl.CostEstimate(
            flops=int(micros * 1.1e9), bytes_accessed=4096, transcendentals=0
        ),
        compiler_params=pltpu.CompilerParams(vmem_limit_bytes=room * 1024 * 1024),
    )(*arrays)


def shaped(*shape):
    return jax.ShapeDtypeStruct(shape, half)


def swap(block, axis, distance):
    count = lax.axis_size(axis)
    return lax.ppermute(block, axis, [(i, i ^ distance) for i in range(count)])


def send_far(block, axis):
    return {0: block} | {k: swap(block, axis, k) for k in range(2, lax.axis_size(axis), 2)}


def send_beside(pieces, axis):
    everything = dict(pieces)
    for k, piece in pieces.items():
        everything[k ^ 1] = swap(piece, axis, 1)
    return [everything[k] for k in sorted(everything)]


def later(value, *others):
    return lax.optimization_barrier((value, *others))[0]


def prepare_kernel(tm_count, info, *refs):
    gain_ref, cut_ref, both_ref, half_ref, normed_ref, stage, frame, sems = refs[5:]
    rows, width = stage.shape[1], stage.shape[2] // tm_count
    query_ref, key_ref, value_ref = (stage.at[i] for i in range(3))
    half_width = half_ref.shape[1]
    side = pl.ds(pl.multiple_of(lax.rem(info[0], 2) * half_width, lanes), half_width)
    sources = (refs[4], *refs[:3], refs[3].at[:, side])
    copies = load(sources, (frame, query_ref, key_ref, value_ref, half_ref), sems)
    copies[0].wait()
    normed_ref[...] = layer_norm(frame[...], gain_ref[...])
    for copy in copies[1:]:
        copy.wait()
    for index in range(tm_count):

        @pl.when(info[0] == index)
        def _():
            columns = slice(index * width, (index + 1) * width)
            cut_ref[:rows, :width] = query_ref[:, columns]
            cut_ref[:rows, width:] = key_ref[:, columns]
            cut_ref[rows:, :width] = value_ref[: rows // 2, columns]
            cut_ref[rows:, width:] = value_ref[rows // 2 :, columns]

    cut_rows, half_rows = cut_ref.shape[0], half_ref.shape[0]
    both_ref[:cut_rows, :] = cut_ref[...]
    both_ref[cut_rows : cut_rows + half_rows, :] = half_ref[:, : 2 * width]
    both_ref[cut_rows + half_rows :, :] = half_ref[:, 2 * width :]


def angle_tables(row_count, model_width, step):
    half_width = model_width // 2
    frequency = jnp.exp(
        jnp.arange(half_width, dtype=jnp.float32) * (-2.0 * math.log(10000.0) / model_width)
    )
    coarse = jnp.arange(row_count // step, dtype=jnp.float32) * step - (row_count // 2 - 1)
    fine = jnp.arange(step, dtype=jnp.float32)
    angles = jnp.concatenate([coarse, fine])[:, None] * frequency[None, :]
    return jnp.sin(angles), jnp.cos(angles)


def relative_kernel(head_size, step, info, sin_ref, cos_ref, position_ref, rel_ref, encoding):
    row_count, model_width = encoding.shape
    half_width = model_width // 2
    coarse_count = row_count // step
    fine_sin, fine_cos = sin_ref[coarse_count:, :], cos_ref[coarse_count:, :]
    for index in range(coarse_count):
        coarse_sin, coarse_cos = sin_ref[index : index + 1, :], cos_ref[index : index + 1, :]
        rows = slice(index * step, (index + 1) * step)
        encoding[rows, :half_width] = (coarse_sin * fine_cos + coarse_cos * fine_sin).astype(half)
        encoding[rows, half_width:] = (coarse_cos * fine_cos - coarse_sin * fine_sin).astype(half)
    projected = lax.dot_general(
        encoding[...], position_ref[...], across, preferred_element_type=jnp.float32
    ).astype(half)
    rel_ref[...] = jnp.zeros_like(rel_ref)
    for h in range(rel_ref.shape[1] // lanes):
        rel_ref[:, h * lanes : h * lanes + head_size] = projected[
            :, h * head_size : (h + 1) * head_size
        ]


def load(sources, targets, sems):
    copies = [
        pltpu.make_async_copy(source, target, sems.at[i])
        for i, (source, target) in enumerate(zip(sources, targets))
    ]
    for copy in copies:
        copy.start()
    return copies


def project_kernel(tm_count, dp_count, head_size, info, *refs):
    normed_refs, refs = refs[:tm_count], refs[tm_count:]
    cut_refs, refs = refs[:dp_count], refs[dp_count:]
    query_ref, key_ref, value_ref, normed, cuts, weight, cut_sems, normed_sems = refs
    block_len = normed.shape[0] // tm_count
    rows, width = cuts.shape[1] * 2 // 3, cuts.shape[2] // 2
    wide = query_ref.shape[1]
    spots = [pl.multiple_of((info[0] ^ k) * block_len, block_len) for k in range(tm_count)]
    sources = [ref.at[: cuts.shape[1], :] for ref in cut_refs]
    cut_copies = load(sources, [cuts.at[k] for k in range(dp_count)], cut_sems)
    normed_copies = load(
        normed_refs, [normed.at[pl.ds(spot, block_len), :] for spot in spots], normed_sems
    )
    weight[...] = jnp.zeros_like(weight)
    value_ref[:block_len, :] = jnp.zeros_like(value_ref[:block_len, :])
    value_ref[(tm_count + 1) * block_len :, :] = jnp.zeros_like(value_ref[:block_len, :])
    for k in range(dp_count):
        cut_copies[k].wait()
        start = pl.multiple_of((info[1] ^ k) * rows, 16)
        for h in range(width // head_size):
            for part in range(2):
                source = part * width + h * head_size
                target = part * wide + h * lanes
                weight[pl.ds(start, rows), target : target + head_size] = cuts[
                    k, :rows, source : source + head_size
                ]
                target = 2 * wide + h * lanes
                weight[
                    pl.ds(start + part * (rows // 2), rows // 2), target : target + head_size
                ] = cuts[k, rows:, source : source + head_size]
    for copy in normed_copies:
        copy.wait()
    shift = slice(block_len, (tm_count + 1) * block_len)
    for part, ref in enumerate((query_ref, key_ref, value_ref.at[shift, :])):
        ref[...] = jnp.dot(
            normed[...],
            weight[:, part * wide : (part + 1) * wide],
            preferred_element_type=jnp.float32,
        ).astype(half)


def softmax_kernel(
    tm_count, info, query, key, relative, content_ref, position_ref, weights_ref, biases
):
    head_count, head_size = weights_ref.shape[1], content_ref.shape[1]
    block_len = weights_ref.shape[2]
    tm_index, valid_len = info[0], info[2]
    biases[...] = jnp.zeros_like(biases)
    for h in range(head_count):
        row = pl.ds(tm_index * head_count + h, 1)
        biases[0:1, h * lanes : h * lanes + head_size] = content_ref[row, :]
        biases[1:2, h * lanes : h * lanes + head_size] = position_ref[row, :]
    scale = 1.0 / math.sqrt(head_size)
    for block in range(tm_count):
        low, high = max(block - 1, 0), min(block + 1, tm_count - 1)
        span = (high - low + 1) * block_len
        first = (low - block + 1) * block_len
        keys = slice(low * block_len, (high + 1) * block_len)
        for h in range(head_count):
            lane = slice(h * lanes, (h + 1) * lanes)
            widened = query[block * block_len : (block + 1) * block_len, lane].astype(jnp.float32)
            with_content = (widened + biases[0:1, lane]).astype(half)
            with_position = (widened + biases[1:2, lane]).astype(half)
            content = lax.dot_general(
                with_content, key[keys, lane], across, preferred_element_type=jnp.float32
            )
            position = lax.dot_general(
                with_position,
                relative[first : first + span + block_len, lane],
                across,
                preferred_element_type=jnp.float32,
            )
            shifted = pltpu.roll(position, span + 1, 1, stride=1, stride_axis=0)[:, :span]
            key_pos = low * block_len + lax.broadcasted_iota(jnp.int32, (1, span), 1)
            scores = jnp.where(key_pos < valid_len, (content + shifted) * scale, masked_score)
            raised = jnp.exp(scores - jnp.max(scores, axis=1, keepdims=True))
            totals = jnp.sum(raised, axis=1, keepdims=True)
            if first > 0:
                weights_ref[block, h, :, :first] = jnp.zeros((block_len, first), half)
            weights_ref[block, h, :, first : first + span] = (raised * (1.0 / totals)).astype(half)
            if first + span < 3 * block_len:
                weights_ref[block, h, :, first + span :] = jnp.zeros(
                    (block_len, 3 * block_len - first - span), half
                )


def mix_values(info, distances, weights_ref, value, context_refs, head_size):
    block_len = weights_ref.shape[2]
    for k, context_ref in zip(distances, context_refs):
        block = info[0] ^ k
        query_pos = block * block_len + lax.broadcasted_iota(jnp.int32, (block_len, 1), 0)
        window = pl.ds(pl.multiple_of(block * block_len, block_len), 3 * block_len)
        width = context_ref.shape[1] // 2
        for h in range(weights_ref.shape[1]):
            context = jnp.dot(
                weights_ref[block, h],
                value[window, h * lanes : (h + 1) * lanes],
                preferred_element_type=jnp.float32,
            )
            context = jnp.where(query_pos < info[2], context, 0.0)[:, :head_size].astype(half)
            for part in range(2):
                lane = part * width + h * head_size
                context_ref[:, lane : lane + head_size] = context[
                    part * (block_len // 2) : (part + 1) * (block_len // 2), :
                ]


def mix_kernel(head_size, distances, info, weights_ref, value, *context_refs):
    rows = weights_ref.shape[2] // 2
    if len(context_refs) == len(distances):
        places = context_refs
    else:
        places = [
            context_refs[i // 2].at[i % 2 * rows : (i % 2 + 1) * rows, :]
            for i in range(len(distances))
        ]
    mix_values(info, distances, weights_ref, value, places, head_size)


def pair_kernel(info, own_ref, beside_ref, pair_ref):
    rows = own_ref.shape[0]
    own = lax.rem(info[1], 2)
    pair_ref[pl.ds(pl.multiple_of(own * rows, 16), rows), :] = own_ref[...]
    first = beside_ref.shape[0] - 2 * rows
    other = pl.ds(pl.multiple_of((1 - own) * rows, 16), rows)
    width = beside_ref.shape[1]
    pair_ref[other, :width] = beside_ref[first : first + rows, :]
    pair_ref[other, width:] = beside_ref[first + rows :, :]


def out_kernel(tm_count, pair_count, info, *refs):
    context_refs, refs = refs[:tm_count], refs[tm_count:]
    pair_refs, refs = refs[: 2 * pair_count], refs[2 * pair_count :]
    frame_ref, out_ref, weight, context, sems = refs
    width = context_refs[0].shape[1] // 2
    rows = pair_refs[0].shape[0]
    half_width = weight.shape[2]
    spots = []
    for k in range(pair_count):
        first = ((info[1] // 2) ^ k) * rows
        source = first // width
        spots.append(pl.multiple_of((source ^ info[0]) * width + first - source * width, 16))
    copies = load(
        pair_refs,
        [weight.at[i // pair_count, pl.ds(spot, rows), :] for i, spot in enumerate(spots * 2)],
        sems,
    )
    for k, ref in enumerate(context_refs):
        for part in range(2):
            context[
                part * (context.shape[0] // 2) : (part + 1) * (context.shape[0] // 2),
                k * width : (k + 1) * width,
            ] = ref[:, part * width : (part + 1) * width]
    for side in range(2):
        for copy in copies[side * pair_count : (side + 1) * pair_count]:
            copy.wait()
        lane = pl.ds(pl.multiple_of((lax.rem(info[0], 2) ^ side) * half_width, lanes), half_width)
        mixed = jnp.dot(context[...], weight[side], preferred_element_type=jnp.float32)
        out_ref[:, lane] = (frame_ref[:, lane].astype(jnp.float32) + mixed).astype(half)


def body_heads(
    frames,
    lengths,
    ln_gain,
    w_query,
    w_key,
    w_value,
    w_output,
    w_position,
    bias_content,
    bias_position,
):
    frame_rows = frames[0]
    block_len, model_width = frame_rows.shape
    head_size = bias_content.shape[1]
    in_rows, inner_width = w_query.shape
    out_rows = w_output.shape[0]
    tm_count, dp_count = lax.axis_size("tm"), lax.axis_size("dp")
    info = jnp.stack((lax.axis_index("tm"), lax.axis_index("dp"), lengths[0])).astype(jnp.int32)
    scalar = (info, scalars)
    width = inner_width // tm_count
    heads = width // head_size
    wide = heads * lanes
    total_len = tm_count * block_len
    row_count = 4 * block_len

    cut, both, half_output, normed_own = call(
        functools.partial(prepare_kernel, tm_count),
        (
            shaped(in_rows // 2 * 3, 2 * width),
            shaped(in_rows // 2 * 3 + 2 * out_rows, 2 * width),
            shaped(out_rows, model_width // 2),
            shaped(block_len, model_width),
        ),
        (
            scalar,
            *((x, far) for x in (w_query, w_key, w_value, w_output, frame_rows)),
            (ln_gain, near),
        ),
        [
            pltpu.VMEM((3, in_rows, inner_width), half),
            pltpu.VMEM((block_len, model_width), half),
            pltpu.SemaphoreType.DMA((5,)),
        ],
        room=56,
    )
    cut_far = send_far(cut, "dp")
    normed_far = send_far(normed_own, "tm")
    cut_pieces = send_beside(cut_far | {0: both}, "dp")
    cut_pieces[0] = cut
    arrived = [cut_far[k] for k in range(2, dp_count, 2)] + cut_pieces[3 : dp_count - 2 : 2]
    pair = call(
        pair_kernel,
        shaped(2 * out_rows, model_width // 2),
        (scalar, (half_output, near), (cut_pieces[1], near)),
        micros=0.5,
    )
    step = 32
    sines, cosines = angle_tables(row_count, model_width, step)
    relative = call(
        functools.partial(relative_kernel, head_size, step),
        shaped(row_count, wide),
        (scalar, (sines, near), (cosines, near), (w_position.T, near)),
        [pltpu.VMEM((row_count, model_width), half)],
        micros=2.0,
    )
    normed_pieces = send_beside(
        {k: later(x, *arrived, relative, pair) for k, x in normed_far.items()}, "tm"
    )
    pairs = send_far(later(pair, *[cut_far[k] for k in range(2, dp_count, 2)]), "dp")
    query, key, value = call(
        functools.partial(project_kernel, tm_count, dp_count, head_size),
        (
            shaped(total_len, wide),
            shaped(total_len, wide),
            shaped(total_len + 2 * block_len, wide),
        ),
        (scalar, *((x, far) for x in normed_pieces), *((x, far) for x in cut_pieces)),
        [
            pltpu.VMEM((total_len, model_width), half),
            pltpu.VMEM((dp_count, in_rows // 2 * 3, 2 * width), half),
            pltpu.VMEM((model_width, 3 * wide), half),
            pltpu.SemaphoreType.DMA((dp_count,)),
            pltpu.SemaphoreType.DMA((tm_count,)),
        ],
        micros=6.0,
    )
    weights = call(
        functools.partial(softmax_kernel, tm_count),
        shaped(tm_count, heads, block_len, 3 * block_len),
        (
            scalar,
            (query, near),
            (key, near),
            (relative, near),
            (bias_content, near),
            (bias_position, near),
        ),
        [pltpu.VMEM((8, wide), jnp.float32)],
        micros=5.0,
    )
    away = range(2, tm_count)
    doubles = call(
        functools.partial(mix_kernel, head_size, away),
        [shaped(block_len, 2 * width)] * (len(away) // 2),
        (scalar, (weights, near), (value, near)),
    )
    received = {k: swap(double, "tm", k) for k, double in zip(away[::2], doubles)}
    own, beside = call(
        functools.partial(mix_kernel, head_size, range(2)),
        [shaped(block_len // 2, 2 * width)] * 2,
        (scalar, (weights, near), (value, near)),
    )
    mine = {0: own, 1: swap(beside, "tm", 1)}
    for k, double in received.items():
        mine[k] = double[: block_len // 2]
        mine[k + 1] = swap(double[block_len // 2 :], "tm", 1)
    own_pairs = [pairs[k] for k in sorted(pairs)]
    other_pairs = [swap(later(x, beside), "tm", 1) for x in own_pairs]
    attended = call(
        functools.partial(out_kernel, tm_count, len(own_pairs)),
        shaped(block_len, model_width),
        (
            scalar,
            *((mine[k], near) for k in range(tm_count)),
            *((x, far) for x in own_pairs + other_pairs),
            (frame_rows, near),
        ),
        [
            pltpu.VMEM((2, inner_width, model_width // 2), half),
            pltpu.VMEM((block_len, inner_width), half),
            pltpu.SemaphoreType.DMA((2 * len(own_pairs),)),
        ],
        micros=2.5,
    )
    return attended[None]


def body(*args):
    tm_count, dp_count = lax.axis_size("tm"), lax.axis_size("dp")
    head_count, head_size = args[-1].shape
    powers = all(n > 1 and n & (n - 1) == 0 for n in (tm_count, dp_count))
    fits = head_size <= lanes and args[3].shape[0] % 32 == 0 and args[6].shape[0] % 16 == 0
    aligned = args[3].shape[1] // tm_count % (2 * args[6].shape[0]) == 0
    if powers and fits and aligned and head_count % tm_count == 0:
        return body_heads(*args)
    return body_blocks(*args)


def solution(mesh):
    placed = (
        P("dp", "tm", None),
        P("dp"),
        P(),
        P("dp", None),
        P("dp", None),
        P("dp", None),
        P("dp", None),
        P(None, "tm"),
        P(),
        P(),
    )
    return jax.shard_map(
        body, mesh=mesh, in_specs=placed, out_specs=P("dp", "tm", None), check_vma=False
    )
```

```python
import functools
import math

import jax
import jax.numpy as jnp
from jax import lax
from jax.experimental import pallas as pl
from jax.experimental.pallas import tpu as pltpu
from jax.sharding import PartitionSpec as P

epsilon = 1e-05
masked_score = -1e30


def padded(block, sides, width):
    for axis, dim in sides:
        count = lax.axis_size(axis)
        forward = [(i, i + 1) for i in range(count - 1)]
        backward = [(target, source) for source, target in forward]
        low = lax.ppermute(
            lax.slice_in_dim(block, block.shape[dim] - width, None, axis=dim), axis, forward
        )
        high = lax.ppermute(lax.slice_in_dim(block, 0, width, axis=dim), axis, backward)
        block = jnp.concatenate([low, block, high], axis=dim)
    return block


def layer_norm(frame_rows, ln_gain):
    widened = frame_rows.astype(jnp.float32)
    row_mean = jnp.mean(widened, axis=-1, keepdims=True)
    centered = widened - row_mean
    row_var = jnp.mean(centered * centered, axis=-1, keepdims=True)
    return (centered * lax.rsqrt(row_var + epsilon) * ln_gain).astype(jnp.bfloat16)


def sinusoid(row_count, model_width):
    offsets = jnp.arange(row_count, dtype=jnp.float32) - (row_count // 2 - 1)
    half_width = model_width // 2
    frequency = jnp.exp(
        jnp.arange(half_width, dtype=jnp.float32) * (-2.0 * math.log(10000.0) / model_width)
    )
    angles = offsets[:, None] * frequency[None, :]
    return jnp.concatenate([jnp.sin(angles), jnp.cos(angles)], axis=1).astype(jnp.bfloat16)


def rel_shift(position_full):
    block_len = position_full.shape[0]
    span_len = position_full.shape[1]
    skewed = position_full.reshape(-1)[: block_len * (span_len - 1)].reshape(
        block_len, span_len - 1
    )
    return skewed[:, block_len - 1 : 4 * block_len - 1]


def attend(
    query_proj, key_rows, value_rows, rel_heads, bias_content, bias_position, valid_len, first_pos
):
    block_len = query_proj.shape[0]
    head_count, head_size = bias_content.shape
    query_pos = first_pos + jnp.arange(block_len, dtype=jnp.int32)
    key_pos = first_pos - block_len + jnp.arange(3 * block_len, dtype=jnp.int32)
    key_valid = (key_pos >= 0) & (key_pos < valid_len)
    query_valid = (query_pos < valid_len).astype(jnp.float32)
    split_query = query_proj.reshape(block_len, head_count, head_size).astype(jnp.float32)
    with_content = (split_query + bias_content[None]).astype(jnp.bfloat16).transpose(1, 0, 2)
    with_position = (split_query + bias_position[None]).astype(jnp.bfloat16).transpose(1, 0, 2)
    key_heads = key_rows.reshape(3 * block_len, head_count, head_size).transpose(1, 0, 2)
    value_heads = value_rows.reshape(3 * block_len, head_count, head_size).transpose(1, 0, 2)
    scale = 1.0 / math.sqrt(head_size)

    def one_head(operands):
        content_query, position_query, key_head, value_head, rel_head = operands
        content = jnp.dot(content_query, key_head.T, preferred_element_type=jnp.float32)
        shifted = rel_shift(jnp.dot(position_query, rel_head.T, preferred_element_type=jnp.float32))
        scores = jnp.where(key_valid[None, :], (content + shifted) * scale, masked_score)
        row_max = jnp.max(scores, axis=1, keepdims=True)
        raised = jnp.exp(scores - row_max)
        totals = jnp.sum(raised, axis=1, keepdims=True)
        weights = (raised / totals).astype(jnp.bfloat16)
        return jnp.dot(weights, value_head, preferred_element_type=jnp.float32)

    context = lax.map(one_head, (with_content, with_position, key_heads, value_heads, rel_heads))
    context = context.transpose(1, 0, 2) * query_valid[:, None, None]
    return context.astype(jnp.bfloat16).reshape(block_len, head_count * head_size)


def column_cut(weight_shard, tm_index, tm_count):
    slice_width = weight_shard.shape[1] // tm_count
    return lax.dynamic_slice_in_dim(weight_shard, tm_index * slice_width, slice_width, 1)


def body_blocks(
    frames,
    lengths,
    ln_gain,
    w_query,
    w_key,
    w_value,
    w_output,
    w_position,
    bias_content,
    bias_position,
):
    frame_rows = frames[0]
    valid_len = lengths[0]
    block_len = frame_rows.shape[0]
    model_width = frame_rows.shape[1]
    head_count, head_size = bias_content.shape
    tm_index = lax.axis_index("tm")
    first_pos = tm_index * block_len
    normed = layer_norm(frame_rows, ln_gain)
    rel_share = jnp.dot(
        sinusoid(4 * block_len, model_width), w_position, preferred_element_type=jnp.float32
    ).astype(jnp.bfloat16)
    relative = lax.all_gather(rel_share, "tm", axis=1, tiled=True)
    rel_heads = relative.reshape(4 * block_len, head_count, head_size).transpose(1, 0, 2)
    tm_count = lax.axis_size("tm")
    slice_query, slice_key, slice_value, slice_output = (
        lax.all_gather(column_cut(w_query, tm_index, tm_count), "dp", axis=0, tiled=True),
        lax.all_gather(column_cut(w_key, tm_index, tm_count), "dp", axis=0, tiled=True),
        lax.all_gather(column_cut(w_value, tm_index, tm_count), "dp", axis=0, tiled=True),
        lax.all_gather(column_cut(w_output, tm_index, tm_count), "dp", axis=0, tiled=True),
    )
    full_query, full_key, full_value, full_output = (
        lax.all_gather(slice_query, "tm", axis=1, tiled=True),
        lax.all_gather(slice_key, "tm", axis=1, tiled=True),
        lax.all_gather(slice_value, "tm", axis=1, tiled=True),
        lax.all_gather(slice_output, "tm", axis=1, tiled=True),
    )
    query_sum = jnp.dot(normed, full_query, preferred_element_type=jnp.float32)
    key_sum = jnp.dot(normed, full_key, preferred_element_type=jnp.float32)
    value_sum = jnp.dot(normed, full_value, preferred_element_type=jnp.float32)
    query_proj = query_sum.astype(jnp.bfloat16)
    key_proj = key_sum.astype(jnp.bfloat16)
    value_proj = value_sum.astype(jnp.bfloat16)
    stacked = jnp.stack((key_proj, value_proj))
    widened = padded(stacked, (("tm", 1),), block_len)
    key_rows = widened[0]
    value_rows = widened[1]
    context = attend(
        query_proj,
        key_rows,
        value_rows,
        rel_heads,
        bias_content,
        bias_position,
        valid_len,
        first_pos,
    )
    mixed_out = jnp.dot(context, full_output, preferred_element_type=jnp.float32)
    attended = (frame_rows.astype(jnp.float32) + mixed_out).astype(jnp.bfloat16)
    return attended[None]


lanes = 128
half = jnp.bfloat16
across = (((1,), (1,)), ((), ()))
near = pl.BlockSpec(memory_space=pltpu.VMEM)
far = pl.BlockSpec(memory_space=pltpu.HBM)
scalars = pl.BlockSpec(memory_space=pltpu.SMEM)


def call(kernel, out_shape, operands, scratch=(), micros=1.0, room=24):
    arrays, specs = zip(*operands)
    return pl.pallas_call(
        kernel,
        out_shape=out_shape,
        in_specs=list(specs),
        out_specs=jax.tree.map(lambda _: near, out_shape),
        scratch_shapes=list(scratch),
        cost_estimate=pl.CostEstimate(
            flops=int(micros * 1.1e9), bytes_accessed=4096, transcendentals=0
        ),
        compiler_params=pltpu.CompilerParams(vmem_limit_bytes=room * 1024 * 1024),
    )(*arrays)


def shaped(*shape):
    return jax.ShapeDtypeStruct(shape, half)


def swap(block, axis, distance):
    count = lax.axis_size(axis)
    return lax.ppermute(block, axis, [(i, i ^ distance) for i in range(count)])


def send_far(block, axis):
    return {0: block} | {k: swap(block, axis, k) for k in range(2, lax.axis_size(axis), 2)}


def send_beside(pieces, axis):
    everything = dict(pieces)
    for k, piece in pieces.items():
        everything[k ^ 1] = swap(piece, axis, 1)
    return [everything[k] for k in sorted(everything)]


def later(value, *others):
    return lax.optimization_barrier((value, *others))[0]


def prepare_kernel(tm_count, info, *refs):
    gain_ref, cut_ref, both_ref, half_ref, normed_ref, stage, frame, sems = refs[5:]
    rows, width = stage.shape[1], stage.shape[2] // tm_count
    query_ref, key_ref, value_ref = (stage.at[i] for i in range(3))
    half_width = half_ref.shape[1]
    side = pl.ds(pl.multiple_of(lax.rem(info[0], 2) * half_width, lanes), half_width)
    sources = (refs[4], *refs[:3], refs[3].at[:, side])
    copies = load(sources, (frame, query_ref, key_ref, value_ref, half_ref), sems)
    copies[0].wait()
    normed_ref[...] = layer_norm(frame[...], gain_ref[...])
    for copy in copies[1:]:
        copy.wait()
    for index in range(tm_count):

        @pl.when(info[0] == index)
        def _():
            columns = slice(index * width, (index + 1) * width)
            cut_ref[:rows, :width] = query_ref[:, columns]
            cut_ref[:rows, width:] = key_ref[:, columns]
            cut_ref[rows:, :width] = value_ref[: rows // 2, columns]
            cut_ref[rows:, width:] = value_ref[rows // 2 :, columns]

    cut_rows, half_rows = cut_ref.shape[0], half_ref.shape[0]
    both_ref[:cut_rows, :] = cut_ref[...]
    both_ref[cut_rows : cut_rows + half_rows, :] = half_ref[:, : 2 * width]
    both_ref[cut_rows + half_rows :, :] = half_ref[:, 2 * width :]


def angle_tables(row_count, model_width, step):
    half_width = model_width // 2
    frequency = jnp.exp(
        jnp.arange(half_width, dtype=jnp.float32) * (-2.0 * math.log(10000.0) / model_width)
    )
    coarse = jnp.arange(row_count // step, dtype=jnp.float32) * step - (row_count // 2 - 1)
    fine = jnp.arange(step, dtype=jnp.float32)
    angles = jnp.concatenate([coarse, fine])[:, None] * frequency[None, :]
    return jnp.sin(angles), jnp.cos(angles)


def relative_kernel(head_size, step, info, sin_ref, cos_ref, position_ref, rel_ref, encoding):
    row_count, model_width = encoding.shape
    half_width = model_width // 2
    coarse_count = row_count // step
    fine_sin, fine_cos = sin_ref[coarse_count:, :], cos_ref[coarse_count:, :]
    for index in range(coarse_count):
        coarse_sin, coarse_cos = sin_ref[index : index + 1, :], cos_ref[index : index + 1, :]
        rows = slice(index * step, (index + 1) * step)
        encoding[rows, :half_width] = (coarse_sin * fine_cos + coarse_cos * fine_sin).astype(half)
        encoding[rows, half_width:] = (coarse_cos * fine_cos - coarse_sin * fine_sin).astype(half)
    projected = lax.dot_general(
        encoding[...], position_ref[...], across, preferred_element_type=jnp.float32
    ).astype(half)
    rel_ref[...] = jnp.zeros_like(rel_ref)
    for h in range(rel_ref.shape[1] // lanes):
        rel_ref[:, h * lanes : h * lanes + head_size] = projected[
            :, h * head_size : (h + 1) * head_size
        ]


def load(sources, targets, sems):
    copies = [
        pltpu.make_async_copy(source, target, sems.at[i])
        for i, (source, target) in enumerate(zip(sources, targets))
    ]
    for copy in copies:
        copy.start()
    return copies


def gather_kernel(tm_count, info, *refs):
    normed, sems = refs[tm_count:]
    block_len = refs[0].shape[0]
    spots = [pl.multiple_of((info[0] ^ k) * block_len, block_len) for k in range(tm_count)]
    targets = [normed.at[pl.ds(spot, block_len), :] for spot in spots]
    for copy in load(refs[:tm_count], targets, sems):
        copy.wait()


def project_kernel(tm_count, dp_count, head_size, info, normed, *refs):
    cut_refs, refs = refs[:dp_count], refs[dp_count:]
    query_ref, key_ref, value_ref, cuts, weight, cut_sems = refs
    block_len = normed.shape[0] // tm_count
    rows, width = cuts.shape[1] * 2 // 3, cuts.shape[2] // 2
    wide = query_ref.shape[1]
    sources = [ref.at[: cuts.shape[1], :] for ref in cut_refs]
    cut_copies = load(sources, [cuts.at[k] for k in range(dp_count)], cut_sems)
    weight[...] = jnp.zeros_like(weight)
    value_ref[:block_len, :] = jnp.zeros_like(value_ref[:block_len, :])
    value_ref[(tm_count + 1) * block_len :, :] = jnp.zeros_like(value_ref[:block_len, :])
    for k in range(dp_count):
        cut_copies[k].wait()
        start = pl.multiple_of((info[1] ^ k) * rows, 16)
        for h in range(width // head_size):
            for part in range(2):
                source = part * width + h * head_size
                target = part * wide + h * lanes
                weight[pl.ds(start, rows), target : target + head_size] = cuts[
                    k, :rows, source : source + head_size
                ]
                target = 2 * wide + h * lanes
                weight[
                    pl.ds(start + part * (rows // 2), rows // 2), target : target + head_size
                ] = cuts[k, rows:, source : source + head_size]
    step = tm_count * block_len
    for start in range(0, tm_count * block_len, step):
        projected = jnp.dot(
            normed[start : start + step, :], weight[...], preferred_element_type=jnp.float32
        ).astype(half)
        query_ref[start : start + step, :] = projected[:, :wide]
        key_ref[start : start + step, :] = projected[:, wide : 2 * wide]
        value_ref[block_len + start : block_len + start + step, :] = projected[:, 2 * wide :]


def softmax_kernel(
    tm_count, info, query, key, relative, content_ref, position_ref, weights_ref, biases
):
    head_count, head_size = weights_ref.shape[1], content_ref.shape[1]
    block_len = weights_ref.shape[2]
    tm_index, valid_len = info[0], info[2]
    biases[...] = jnp.zeros_like(biases)
    for h in range(head_count):
        row = pl.ds(tm_index * head_count + h, 1)
        biases[0:1, h * lanes : h * lanes + head_size] = content_ref[row, :]
        biases[1:2, h * lanes : h * lanes + head_size] = position_ref[row, :]
    scale = 1.0 / math.sqrt(head_size)
    for block in range(tm_count):
        low, high = max(block - 1, 0), min(block + 1, tm_count - 1)
        span = (high - low + 1) * block_len
        first = (low - block + 1) * block_len
        keys = slice(low * block_len, (high + 1) * block_len)
        for h in range(head_count):
            lane = slice(h * lanes, (h + 1) * lanes)
            widened = query[block * block_len : (block + 1) * block_len, lane].astype(jnp.float32)
            with_content = (widened + biases[0:1, lane]).astype(half)
            with_position = (widened + biases[1:2, lane]).astype(half)
            content = lax.dot_general(
                with_content, key[keys, lane], across, preferred_element_type=jnp.float32
            )
            position = lax.dot_general(
                with_position,
                relative[first : first + span + block_len, lane],
                across,
                preferred_element_type=jnp.float32,
            )
            shifted = pltpu.roll(position, span + 1, 1, stride=1, stride_axis=0)[:, :span]
            key_pos = low * block_len + lax.broadcasted_iota(jnp.int32, (1, span), 1)
            scores = jnp.where(key_pos < valid_len, (content + shifted) * scale, masked_score)
            raised = jnp.exp(scores - jnp.max(scores, axis=1, keepdims=True))
            totals = jnp.sum(raised, axis=1, keepdims=True)
            if first > 0:
                weights_ref[block, h, :, :first] = jnp.zeros((block_len, first), half)
            weights_ref[block, h, :, first : first + span] = (raised * (1.0 / totals)).astype(half)
            if first + span < 3 * block_len:
                weights_ref[block, h, :, first + span :] = jnp.zeros(
                    (block_len, 3 * block_len - first - span), half
                )


def mix_values(info, distances, weights_ref, value, context_refs, head_size):
    block_len = weights_ref.shape[2]
    for k, context_ref in zip(distances, context_refs):
        block = info[0] ^ k
        query_pos = block * block_len + lax.broadcasted_iota(jnp.int32, (block_len, 1), 0)
        window = pl.ds(pl.multiple_of(block * block_len, block_len), 3 * block_len)
        width = context_ref.shape[1] // 2
        for h in range(weights_ref.shape[1]):
            context = jnp.dot(
                weights_ref[block, h],
                value[window, h * lanes : (h + 1) * lanes],
                preferred_element_type=jnp.float32,
            )
            context = jnp.where(query_pos < info[2], context, 0.0)[:, :head_size].astype(half)
            for part in range(2):
                lane = part * width + h * head_size
                context_ref[:, lane : lane + head_size] = context[
                    part * (block_len // 2) : (part + 1) * (block_len // 2), :
                ]


def mix_kernel(head_size, distances, info, weights_ref, value, *context_refs):
    rows = weights_ref.shape[2] // 2
    if len(context_refs) == len(distances):
        places = context_refs
    else:
        places = [
            context_refs[i // 2].at[i % 2 * rows : (i % 2 + 1) * rows, :]
            for i in range(len(distances))
        ]
    mix_values(info, distances, weights_ref, value, places, head_size)


def pair_kernel(info, own_ref, beside_ref, pair_ref):
    rows = own_ref.shape[0]
    own = lax.rem(info[1], 2)
    pair_ref[pl.ds(pl.multiple_of(own * rows, 16), rows), :] = own_ref[...]
    first = beside_ref.shape[0] - 2 * rows
    other = pl.ds(pl.multiple_of((1 - own) * rows, 16), rows)
    width = beside_ref.shape[1]
    pair_ref[other, :width] = beside_ref[first : first + rows, :]
    pair_ref[other, width:] = beside_ref[first + rows :, :]


def out_kernel(tm_count, pair_count, info, *refs):
    context_refs, refs = refs[:tm_count], refs[tm_count:]
    pair_refs, refs = refs[: 2 * pair_count], refs[2 * pair_count :]
    frame_ref, out_ref, weight, context, sems = refs
    width = context_refs[0].shape[1] // 2
    rows = pair_refs[0].shape[0]
    half_width = weight.shape[2]
    spots = []
    for k in range(pair_count):
        first = ((info[1] // 2) ^ k) * rows
        source = first // width
        spots.append(pl.multiple_of((source ^ info[0]) * width + first - source * width, 16))
    copies = load(
        pair_refs,
        [weight.at[i // pair_count, pl.ds(spot, rows), :] for i, spot in enumerate(spots * 2)],
        sems,
    )
    for k, ref in enumerate(context_refs):
        for part in range(2):
            context[
                part * (context.shape[0] // 2) : (part + 1) * (context.shape[0] // 2),
                k * width : (k + 1) * width,
            ] = ref[:, part * width : (part + 1) * width]
    for side in range(2):
        for copy in copies[side * pair_count : (side + 1) * pair_count]:
            copy.wait()
        lane = pl.ds(pl.multiple_of((lax.rem(info[0], 2) ^ side) * half_width, lanes), half_width)
        mixed = jnp.dot(context[...], weight[side], preferred_element_type=jnp.float32)
        out_ref[:, lane] = (frame_ref[:, lane].astype(jnp.float32) + mixed).astype(half)


def body_heads(
    frames,
    lengths,
    ln_gain,
    w_query,
    w_key,
    w_value,
    w_output,
    w_position,
    bias_content,
    bias_position,
):
    frame_rows = frames[0]
    block_len, model_width = frame_rows.shape
    head_size = bias_content.shape[1]
    in_rows, inner_width = w_query.shape
    out_rows = w_output.shape[0]
    tm_count, dp_count = lax.axis_size("tm"), lax.axis_size("dp")
    info = jnp.stack((lax.axis_index("tm"), lax.axis_index("dp"), lengths[0])).astype(jnp.int32)
    scalar = (info, scalars)
    width = inner_width // tm_count
    heads = width // head_size
    wide = heads * lanes
    total_len = tm_count * block_len
    row_count = 4 * block_len

    cut, both, half_output, normed_own = call(
        functools.partial(prepare_kernel, tm_count),
        (
            shaped(in_rows // 2 * 3, 2 * width),
            shaped(in_rows // 2 * 3 + 2 * out_rows, 2 * width),
            shaped(out_rows, model_width // 2),
            shaped(block_len, model_width),
        ),
        (
            scalar,
            *((x, far) for x in (w_query, w_key, w_value, w_output, frame_rows)),
            (ln_gain, near),
        ),
        [
            pltpu.VMEM((3, in_rows, inner_width), half),
            pltpu.VMEM((block_len, model_width), half),
            pltpu.SemaphoreType.DMA((5,)),
        ],
        room=56,
    )
    cut_far = send_far(cut, "dp")
    normed_far = send_far(normed_own, "tm")
    cut_pieces = send_beside(cut_far | {0: both}, "dp")
    cut_pieces[0] = cut
    arrived = [cut_far[k] for k in range(2, dp_count, 2)] + cut_pieces[3 : dp_count - 2 : 2]
    pair = call(
        pair_kernel,
        shaped(2 * out_rows, model_width // 2),
        (scalar, (half_output, near), (cut_pieces[1], near)),
        micros=0.5,
    )
    step = 32
    sines, cosines = angle_tables(row_count, model_width, step)
    relative = call(
        functools.partial(relative_kernel, head_size, step),
        shaped(row_count, wide),
        (scalar, (sines, near), (cosines, near), (w_position.T, near)),
        [pltpu.VMEM((row_count, model_width), half)],
        micros=2.0,
    )
    normed_pieces = send_beside(
        {k: later(x, *arrived, relative, pair) for k, x in normed_far.items()}, "tm"
    )
    pairs = send_far(later(pair, *[cut_far[k] for k in range(2, dp_count, 2)]), "dp")
    normed = call(
        functools.partial(gather_kernel, tm_count),
        shaped(total_len, model_width),
        (scalar, *((x, far) for x in normed_pieces)),
        [pltpu.SemaphoreType.DMA((tm_count,))],
        micros=2.0,
    )
    query, key, value = call(
        functools.partial(project_kernel, tm_count, dp_count, head_size),
        (
            shaped(total_len, wide),
            shaped(total_len, wide),
            shaped(total_len + 2 * block_len, wide),
        ),
        (scalar, (normed, near), *((x, far) for x in cut_pieces)),
        [
            pltpu.VMEM((dp_count, in_rows // 2 * 3, 2 * width), half),
            pltpu.VMEM((model_width, 3 * wide), half),
            pltpu.SemaphoreType.DMA((dp_count,)),
        ],
        micros=6.0,
    )
    weights = call(
        functools.partial(softmax_kernel, tm_count),
        shaped(tm_count, heads, block_len, 3 * block_len),
        (
            scalar,
            (query, near),
            (key, near),
            (relative, near),
            (bias_content, near),
            (bias_position, near),
        ),
        [pltpu.VMEM((8, wide), jnp.float32)],
        micros=5.0,
    )
    away = range(2, tm_count)
    doubles = call(
        functools.partial(mix_kernel, head_size, away),
        [shaped(block_len, 2 * width)] * (len(away) // 2),
        (scalar, (weights, near), (value, near)),
    )
    received = {k: swap(double, "tm", k) for k, double in zip(away[::2], doubles)}
    own, beside = call(
        functools.partial(mix_kernel, head_size, range(2)),
        [shaped(block_len // 2, 2 * width)] * 2,
        (scalar, (weights, near), (value, near)),
    )
    mine = {0: own, 1: swap(beside, "tm", 1)}
    for k, double in received.items():
        mine[k] = double[: block_len // 2]
        mine[k + 1] = swap(double[block_len // 2 :], "tm", 1)
    own_pairs = [pairs[k] for k in sorted(pairs)]
    other_pairs = [swap(later(x, beside), "tm", 1) for x in own_pairs]
    attended = call(
        functools.partial(out_kernel, tm_count, len(own_pairs)),
        shaped(block_len, model_width),
        (
            scalar,
            *((mine[k], near) for k in range(tm_count)),
            *((x, far) for x in own_pairs + other_pairs),
            (frame_rows, near),
        ),
        [
            pltpu.VMEM((2, inner_width, model_width // 2), half),
            pltpu.VMEM((block_len, inner_width), half),
            pltpu.SemaphoreType.DMA((2 * len(own_pairs),)),
        ],
        micros=2.5,
    )
    return attended[None]


def body(*args):
    tm_count, dp_count = lax.axis_size("tm"), lax.axis_size("dp")
    head_count, head_size = args[-1].shape
    powers = all(n > 1 and n & (n - 1) == 0 for n in (tm_count, dp_count))
    fits = head_size <= lanes and args[3].shape[0] % 32 == 0 and args[6].shape[0] % 16 == 0
    aligned = args[3].shape[1] // tm_count % (2 * args[6].shape[0]) == 0
    if powers and fits and aligned and head_count % tm_count == 0:
        return body_heads(*args)
    return body_blocks(*args)


def solution(mesh):
    placed = (
        P("dp", "tm", None),
        P("dp"),
        P(),
        P("dp", None),
        P("dp", None),
        P("dp", None),
        P("dp", None),
        P(None, "tm"),
        P(),
        P(),
    )
    return jax.shard_map(
        body, mesh=mesh, in_specs=placed, out_specs=P("dp", "tm", None), check_vma=False
    )
```
